32 devices in a mesh: row: 4 (over y, core), col: 8 (over z, x).
Axes of the slice: x: 2, y: 2, z: 4, core: 2. Of those that a mesh axis runs over, the one named last changes fastest.
Arguments:
- activations: float32 [4096, 2048], P('row', 'col'), may hold values from -6 to 6
- cotangent: float32 [4096, 2048], P('row', 'col'), may hold values from -6 to 6
- lengths: int32 [4], P('row'), may hold values from 256 to 1024, as said below
- first_gain: float32 [2, 2048], P(None, 'col'), may hold values from 0.5 to 1.5
- first_shift: float32 [2, 2048], P(None, 'col'), may hold values from -1.75 to 1.75
- joined_weight: float32 [2, 2048, 6144], P(None, 'row', 'col'), may hold values from -0.125 to 0.125
- query_bias: float32 [2, 2048], P(None, 'col'), may hold values from -1.75 to 1.75
- value_bias: float32 [2, 2048], P(None, 'col'), may hold values from -1.75 to 1.75
- output_weight: float32 [2, 2048, 2048], P(None, 'col', 'row'), may hold values from -0.5 to 0.5
- output_bias: float32 [2, 2048], P(None, 'col'), may hold values from -1.75 to 1.75
- second_gain: float32 [2, 2048], P(None, 'col'), may hold values from 0.5 to 1.5
- second_shift: float32 [2, 2048], P(None, 'col'), may hold values from -1.75 to 1.75
- up_weight: float32 [2, 2048, 8192], P(None, 'row', 'col'), may hold values from -0.125 to 0.125
- up_bias: float32 [2, 8192], P(None, 'col'), may hold values from -1.75 to 1.75
- down_weight: float32 [2, 8192, 2048], P(None, 'col', 'row'), may hold values from -0.0625 to 0.0625
- down_bias: float32 [2, 2048], P(None, 'col'), may hold values from -1.75 to 1.75
Outputs:
- result: float32 [4096, 2048], P('row', 'col')
- input_grad: float32 [4096, 2048], P('row', 'col')
- first_gain_grad: float32 [2, 2048], P(None, 'col')
- first_shift_grad: float32 [2, 2048], P(None, 'col')
- joined_weight_grad: float32 [2, 2048, 6144], P(None, 'row', 'col')
- query_bias_grad: float32 [2, 2048], P(None, 'col')
- value_bias_grad: float32 [2, 2048], P(None, 'col')
- output_weight_grad: float32 [2, 2048, 2048], P(None, 'col', 'row')
- output_bias_grad: float32 [2, 2048], P(None, 'col')
- second_gain_grad: float32 [2, 2048], P(None, 'col')
- second_shift_grad: float32 [2, 2048], P(None, 'col')
- up_weight_grad: float32 [2, 2048, 8192], P(None, 'row', 'col')
- up_bias_grad: float32 [2, 8192], P(None, 'col')
- down_weight_grad: float32 [2, 8192, 2048], P(None, 'col', 'row')
- down_bias_grad: float32 [2, 2048], P(None, 'col')
The draws below stay inside these ranges and needn't reach their ends.
Inputs may be any that keep to these rules, and one draw needn't show every extreme that they name: `lengths`: each slot's length lies between 256 and 1024; in every draw some slot is exactly 1024 long and some exactly 256.
All inputs are finite; a program needn't handle non-finite values.
Results may differ from the reference program's by a relative error of at most 0.015.
Values may be sent and summed in bfloat16 or wider, within the bound.
No kernel may reach another device: no remote copies, remote signals or barrier semaphores. Data moves between devices by JAX's collectives and lax.ppermute only.
A program may use at most 256 MiB of HBM per device.

```python
import math
import jax
import jax.numpy as jnp
from jax import lax

D = 2048
HEADS = 16
HEAD_DIM = 128
FF = 8192
LAYERS = 2
SLOT = 1024
MIN_LEN = 256
SLOTS = 4
TOKENS = 4096


def draw_lengths(key, part):
    key = jax.random.fold_in(key, 11)
    first, second = jax.random.split(key, 2)
    values = jax.random.randint(first, (SLOTS,), MIN_LEN, SLOT + 1)
    order = jax.random.permutation(second, SLOTS)
    values = values.at[order[0]].set(SLOT)
    values = values.at[order[1]].set(MIN_LEN)
    return values.astype(jnp.int32)


def steps_of(rng, shape, cuts, least, top_value):
    factor_of = 1.0
    for dim, blocks in cuts:
        draws = jax.random.uniform(jax.random.fold_in(jax.random.fold_in(rng, 6), dim), (blocks,), jnp.float32, least / len(cuts), top_value / len(cuts))
        factor_of = factor_of * jnp.repeat(jnp.exp(draws), shape[dim] // blocks).reshape((-1,) + (1,) * (len(shape) - 1 - dim))
    return factor_of


def normal_values(rng, extent, spread, most, cuts=(), held_as=jnp.bfloat16):
    drawn = spread * jax.random.normal(rng, extent, jnp.float32)
    if cuts:
        drawn = drawn * steps_of(rng, extent, cuts, -0.22, 0.18)
    return jnp.clip(drawn, -most, most).astype(held_as)


def setup_inputs(seed: int = 0) -> dict:
    seeds = jax.random.split(jax.random.key(seed), 17)
    activations = normal_values(seeds[0], (TOKENS, D), 1.0, 6.0, ((0, 4), (1, 8)), jnp.float32)
    cotangent = normal_values(seeds[1], (TOKENS, D), 1.0, 6.0, ((0, 4), (1, 8)), jnp.float32)
    lengths = draw_lengths(jax.random.fold_in(seeds[16], 71), 0)
    first_gain = jnp.clip(1.0 + 0.1 * jax.random.normal(seeds[3], (LAYERS, D), jnp.float32), 0.5, 1.5)
    first_shift = normal_values(seeds[4], (LAYERS, D), 0.3, 1.75, ((1, 8),), jnp.float32)
    joined_weight = normal_values(seeds[5], (LAYERS, D, 3 * D), D ** -0.5, 0.125, ((1, 4), (2, 8)), jnp.float32)
    query_bias = normal_values(seeds[6], (LAYERS, D), 0.3, 1.75, ((1, 8),), jnp.float32)
    value_bias = normal_values(seeds[7], (LAYERS, D), 0.3, 1.75, ((1, 8),), jnp.float32)
    output_weight = normal_values(seeds[8], (LAYERS, D, D), (D // 16) ** -0.5, 0.5, ((1, 8), (2, 4)), jnp.float32)
    output_bias = normal_values(seeds[9], (LAYERS, D), 0.3, 1.75, ((1, 8),), jnp.float32)
    second_gain = jnp.clip(1.0 + 0.1 * jax.random.normal(seeds[10], (LAYERS, D), jnp.float32), 0.5, 1.5)
    second_shift = normal_values(seeds[11], (LAYERS, D), 0.3, 1.75, ((1, 8),), jnp.float32)
    up_weight = normal_values(seeds[12], (LAYERS, D, FF), D ** -0.5, 0.125, ((1, 4), (2, 8)), jnp.float32)
    up_bias = normal_values(seeds[13], (LAYERS, FF), 0.3, 1.75, ((1, 8),), jnp.float32)
    down_weight = normal_values(seeds[14], (LAYERS, FF, D), FF ** -0.5, 0.0625, ((1, 8), (2, 4)), jnp.float32)
    down_bias = normal_values(seeds[15], (LAYERS, D), 0.3, 1.75, ((1, 8),), jnp.float32)
    return dict(activations=activations, cotangent=cotangent, lengths=lengths, first_gain=first_gain, first_shift=first_shift, joined_weight=joined_weight, query_bias=query_bias, value_bias=value_bias, output_weight=output_weight, output_bias=output_bias, second_gain=second_gain, second_shift=second_shift, up_weight=up_weight, up_bias=up_bias, down_weight=down_weight, down_bias=down_bias)


@jax.custom_vjp
def low(v):
    return lax.optimization_barrier(v.astype(jnp.bfloat16)).astype(jnp.float32)

@jax.custom_vjp
def low_back(v):
    return v

def low_keep(v):
    return (low(v), None)

def low_pass(kept, grad):
    return (grad,)

def back_keep(v):
    return (v, None)

def back_low(kept, grad):
    return (low(grad),)
low.defvjp(low_keep, low_pass)
low_back.defvjp(back_keep, back_low)
norm_eps = 1e-05
masked_score = -1e+30
highest = lax.Precision.HIGHEST

def layer_norm(value, gain, shift):
    mean = lax.optimization_barrier(jnp.mean(value, axis=-1, keepdims=True))
    variance = lax.optimization_barrier(jnp.mean(value * value, axis=-1, keepdims=True)) - mean * mean
    return (value - mean) * lax.rsqrt(variance + norm_eps) * gain + shift

def slot_attention(pieces):
    query, key, value, length = pieces
    position = jnp.arange(SLOT)
    distance = (position[:, None] - position[None, :]).astype(jnp.float32)
    allowed = (position[None, :] <= position[:, None]) & (position[None, :] < length)
    slopes = jnp.exp2(-8.0 * (jnp.arange(HEADS) + 1).astype(jnp.float32) / HEADS)
    scores = jnp.einsum('qhd,khd->hqk', query, key, precision=highest) * (1.0 / math.sqrt(HEAD_DIM))
    scores = scores - slopes[:, None, None] * distance[None]
    scores = low_back(jnp.where(allowed[None], scores, masked_score))
    chances = jax.nn.softmax(scores, axis=-1)
    return jnp.einsum('hqk,khd->qhd', low(chances), value, precision=highest)

def forward(residual, lengths, first_gain, first_shift, joined_weight, query_bias, value_bias, output_weight, output_bias, second_gain, second_shift, up_weight, up_bias, down_weight, down_bias):
    attend = jax.checkpoint(slot_attention)
    for layer in range(LAYERS):
        normed = low(layer_norm(residual, first_gain[layer], first_shift[layer]))
        joined = jnp.dot(normed, low(joined_weight[layer]), precision=highest).reshape(TOKENS, HEADS, 3, HEAD_DIM)
        query = low(low_back(joined[:, :, 0] + query_bias[layer].reshape(HEADS, HEAD_DIM)))
        key = low(low_back(joined[:, :, 1]))
        value = low(low_back(joined[:, :, 2] + value_bias[layer].reshape(HEADS, HEAD_DIM)))
        context = lax.map(attend, (query.reshape(SLOTS, SLOT, HEADS, HEAD_DIM), key.reshape(SLOTS, SLOT, HEADS, HEAD_DIM), value.reshape(SLOTS, SLOT, HEADS, HEAD_DIM), lengths))
        context = low(low_back(context.reshape(TOKENS, D)))
        residual = residual + low_back(jnp.dot(context, low(output_weight[layer]), precision=highest)) + output_bias[layer]
        normed = low(layer_norm(residual, second_gain[layer], second_shift[layer]))
        upper = low_back(jnp.dot(normed, low(up_weight[layer]), precision=highest) + up_bias[layer])
        activated = low(jax.nn.gelu(upper, approximate=True))
        residual = residual + low_back(jnp.dot(activated, low(down_weight[layer]), precision=highest)) + down_bias[layer]
    return residual

def reference(activations, cotangent, lengths, first_gain, first_shift, joined_weight, query_bias, value_bias, output_weight, output_bias, second_gain, second_shift, up_weight, up_bias, down_weight, down_bias):
    valid = (jnp.arange(SLOT)[None, :] < lengths[:, None]).reshape(TOKENS, 1).astype(jnp.float32)

    def run(residual, *weights):
        return forward(residual, lengths, *weights)
    result, pullback = jax.vjp(run, activations, first_gain, first_shift, joined_weight, query_bias, value_bias, output_weight, output_bias, second_gain, second_shift, up_weight, up_bias, down_weight, down_bias)
    grads = pullback(cotangent * valid)
    return (result, grads[0], grads[1], grads[2], grads[3], grads[4], grads[5], grads[6], grads[7], grads[8], grads[9], grads[10], grads[11], grads[12], grads[13])
```

```python
import functools
import math

import jax
import jax.numpy as jnp
from jax import lax
from jax.experimental import pallas as pl
from jax.experimental.pallas import tpu as pltpu
from jax.sharding import Mesh
from jax.sharding import PartitionSpec as P

HEADS = 16
HEAD_DIM = 128
PAD = 16
LANES = 128

norm_eps = 1e-05
masked_score = -1e30

F32 = jnp.float32
BF16 = jnp.bfloat16


def gelu_tanh(value):
    return jax.nn.gelu(value, approximate=True)


def ring_size():
    return lax.axis_size("t")


def ring(value, k):
    if k == 0:
        return value
    return lax.ppermute(value, "t", [(i, i ^ k) for i in range(ring_size())])


def partner(value):
    return lax.ppermute(value, "c", [(0, 1), (1, 0)])


def far(value):
    return lax.ppermute(value, "zh", [(0, 1), (1, 0)])


def swap_roles(value):
    return lax.ppermute(value, ("c", "zh"), [(0, 0), (1, 2), (2, 1), (3, 3)])


def block_index():
    return lax.axis_index("c") * ring_size() + lax.axis_index("t")


def slot_blocks():
    return (jnp.arange(2 * ring_size(), dtype=jnp.int32) ^ block_index()).astype(jnp.int32)


def gather_slots(value):
    mine = [ring(value, k) for k in range(ring_size())]
    return mine + [partner(v) for v in mine]


def scatter_slots(mine, other):
    got = partner(other)
    pair = mine.astype(F32) + got.astype(F32)
    total = pair[0]
    for k in range(1, ring_size()):
        total = total + ring(pair[k].astype(BF16), k).astype(F32)
    return total


def rows_of(column):
    return column.reshape(-1, LANES)


def packed(value, rows, width):
    extra = jnp.zeros((PAD, width), value.dtype)
    extra = lax.dynamic_update_slice(extra, rows.astype(value.dtype), (0, 0))
    return jnp.concatenate([value, extra], axis=0)


def assemble_norm_kernel(slots, width, blocks_ref, *refs):
    shards = refs[:slots]
    means_ref, spread_ref, gain_ref, shift_ref, own_ref = refs[slots : slots + 5]
    out_ref, centred_ref, inverse_ref = refs[slots + 5 :]
    f = shards[0].shape[1]
    offsets = lax.dot_general(
        means_ref[0].astype(BF16),
        spread_ref[...],
        (((0,), (0,)), ((), ())),
        preferred_element_type=F32,
    )
    values = [shards[s][...].astype(F32) + offsets[:, s * f : (s + 1) * f] for s in range(slots)]
    total = values[0]
    for v in values[1:]:
        total = total + v
    mean = jnp.sum(total, axis=1, keepdims=True) / width
    values = [v - mean for v in values]
    squares = values[0] * values[0]
    for v in values[1:]:
        squares = squares + v * v
    inverse = lax.rsqrt(jnp.sum(squares, axis=1, keepdims=True) / width + norm_eps)
    for s in range(slots):
        block = blocks_ref[s]
        normed = values[s] * inverse * gain_ref[block] + shift_ref[block]
        out_ref[:, pl.ds(pl.multiple_of(block * f, f), f)] = normed.astype(BF16)
    centred_ref[...] = (own_ref[...] - mean) * inverse
    inverse_ref[...] = jnp.broadcast_to(inverse, inverse_ref.shape)


def assemble_norm(shards, own, gain, shift):
    slots = len(shards)
    tokens, f = own.shape
    width = slots * f
    groups = tokens // LANES
    means = jnp.stack([s[tokens : tokens + groups, :LANES] for s in shards], axis=1).astype(F32)
    spread = jnp.repeat(jnp.eye(slots, dtype=BF16), f, axis=1)
    tile = LANES
    whole = lambda shape: pl.BlockSpec(shape, lambda g, b: (0,) * len(shape))
    return pl.pallas_call(
        functools.partial(assemble_norm_kernel, slots, width),
        grid_spec=pltpu.PrefetchScalarGridSpec(
            num_scalar_prefetch=1,
            grid=(tokens // tile,),
            in_specs=[pl.BlockSpec((tile, f), lambda g, b: (g, 0))] * slots
            + [
                pl.BlockSpec((1, slots, LANES), lambda g, b: (g, 0, 0)),
                whole((slots, width)),
                whole((slots, 1, f)),
                whole((slots, 1, f)),
                pl.BlockSpec((tile, f), lambda g, b: (g, 0)),
            ],
            out_specs=[
                pl.BlockSpec((tile, width), lambda g, b: (g, 0)),
                pl.BlockSpec((tile, f), lambda g, b: (g, 0)),
                pl.BlockSpec((tile, LANES), lambda g, b: (g, 0)),
            ],
        ),
        out_shape=[
            jax.ShapeDtypeStruct((tokens, width), BF16),
            jax.ShapeDtypeStruct((tokens, f), F32),
            jax.ShapeDtypeStruct((tokens, LANES), F32),
        ],
        compiler_params=pltpu.CompilerParams(vmem_limit_bytes=24 * 2**20),
        cost_estimate=pl.CostEstimate(
            flops=12 * tokens * width, bytes_accessed=6 * tokens * width, transcendentals=tokens
        ),
        name="assemble_norm",
    )(
        slot_blocks(),
        *shards,
        means,
        spread,
        gain.reshape(slots, 1, f),
        shift.reshape(slots, 1, f),
        own,
    )


def assemble_kernel(slots, blocks_ref, *refs):
    out_ref = refs[slots]
    f = refs[0].shape[1]
    for s in range(slots):
        out_ref[:, pl.ds(pl.multiple_of(blocks_ref[s] * f, f), f)] = refs[s][...]


def assemble(shards):
    slots = len(shards)
    tokens, f = shards[0].shape
    tile = min(tokens, 256)
    return pl.pallas_call(
        functools.partial(assemble_kernel, slots),
        grid_spec=pltpu.PrefetchScalarGridSpec(
            num_scalar_prefetch=1,
            grid=(tokens // tile,),
            in_specs=[pl.BlockSpec((tile, f), lambda g, b: (g, 0))] * slots,
            out_specs=pl.BlockSpec((tile, slots * f), lambda g, b: (g, 0)),
        ),
        out_shape=jax.ShapeDtypeStruct((tokens, slots * f), shards[0].dtype),
        compiler_params=pltpu.CompilerParams(vmem_limit_bytes=24 * 2**20),
        cost_estimate=pl.CostEstimate(
            flops=0, bytes_accessed=4 * tokens * slots * f, transcendentals=0
        ),
        name="assemble",
    )(slot_blocks(), *shards)


def slot_matmul_kernel(transposed, tile, blocks_ref, x_ref, w_ref, extra_ref, out_ref):
    tokens = x_ref.shape[0]
    w = w_ref[...].reshape(w_ref.shape[-2:])
    dims = (((1,), (1 if transposed else 0,)), ((), ()))

    @pl.loop(0, tokens // tile)
    def _(g):
        at = pl.ds(pl.multiple_of(g * tile, tile), tile)
        out_ref[0, at, :] = lax.dot_general(
            x_ref[at, :], w, dims, preferred_element_type=F32
        ).astype(BF16)

    out_ref[0, tokens:, :] = extra_ref[...]


def slot_matmul(x, w, extra, other, transposed):
    tokens, depth = x.shape
    n = ring_size()
    f = extra.shape[1]
    blocks = slot_blocks()
    blocks = blocks[n:] if other else blocks[:n]
    if transposed:
        w_spec = pl.BlockSpec((f, depth), lambda k, b: (b[k], 0))
    else:
        per = w.shape[2] // f
        w_spec = pl.BlockSpec((1, depth, f), lambda k, b: (b[k] // per, 0, b[k] % per))
    tile = min(tokens, 256)
    return pl.pallas_call(
        functools.partial(slot_matmul_kernel, transposed, tile),
        grid_spec=pltpu.PrefetchScalarGridSpec(
            num_scalar_prefetch=1,
            grid=(n,),
            in_specs=[
                pl.BlockSpec((tokens, depth), lambda k, b: (0, 0)),
                w_spec,
                pl.BlockSpec((PAD, f), lambda k, b: (0, 0)),
            ],
            out_specs=pl.BlockSpec((1, tokens + PAD, f), lambda k, b: (k, 0, 0)),
        ),
        out_shape=jax.ShapeDtypeStruct((n, tokens + PAD, f), BF16),
        compiler_params=pltpu.CompilerParams(vmem_limit_bytes=24 * 2**20),
        cost_estimate=pl.CostEstimate(
            flops=2 * tokens * depth * n * f,
            bytes_accessed=2 * (tokens * depth + n * f * (depth + tokens)),
            transcendentals=0,
        ),
        name="slot_matmul",
    )(blocks, x, w, extra)


def column_sum(x, w, extra, transposed):
    other = slot_matmul(x, w, extra, True, transposed)
    mine = slot_matmul(x, w, extra, False, transposed)
    return scatter_slots(mine, other)


def gather_weight(weight):
    same = lax.axis_index("c") == lax.axis_index("zh")
    first = lax.axis_index("c") == 0
    own = weight.astype(BF16)
    received = far(own)
    keep = jnp.where(same, own, received)
    got = partner(jnp.where(same, received, own))
    pair = jnp.stack([jnp.where(first, keep, got), jnp.where(first, got, keep)])
    return lax.all_gather(pair, "rh", axis=0, tiled=True)


def scatter_weight(term):
    same = lax.axis_index("c") == lax.axis_index("zh")
    first = lax.axis_index("c") == 0
    pair = lax.psum_scatter(term.astype(BF16), "rh", scatter_dimension=0, tiled=True)
    mine = jnp.where(first, pair[0], pair[1])
    got = partner(jnp.where(first, pair[1], pair[0]))
    keep = jnp.where(same, mine, got)
    received = far(jnp.where(same, got, mine))
    return keep.astype(F32) + received.astype(F32)


def slot_scores(query, key, lengths, slopes):
    slot_count = lengths.shape[0]
    span = query.shape[0] // slot_count
    heads = query.shape[1]
    depth = query.shape[2]
    query_slots = query.reshape(slot_count, span, heads, depth)
    key_slots = key.reshape(slot_count, span, heads, depth)
    position = jnp.arange(span)
    distance = (position[:, None] - position[None, :]).astype(F32)
    allowed = (position[None, None, :] <= position[None, :, None]) & (
        position[None, None, :] < lengths[:, None, None]
    )
    scores = jnp.einsum(
        "sqhd,skhd->shqk", query_slots, key_slots, preferred_element_type=F32
    ) * (1.0 / math.sqrt(depth))
    scores = scores - slopes[None, :, None, None] * distance[None, None]
    return jnp.where(allowed[:, None], scores, masked_score)


def attention_forward(query, key, value, lengths, slopes):
    tokens, heads, depth = query.shape
    slot_count = lengths.shape[0]
    scores = slot_scores(query, key, lengths, slopes)
    highest_score = jnp.max(scores, axis=-1, keepdims=True)
    raised = jnp.exp(scores - highest_score)
    total = jnp.sum(raised, axis=-1, keepdims=True)
    chances = raised / total
    log_total = highest_score[..., 0] + jnp.log(total[..., 0])
    value_slots = value.reshape(slot_count, tokens // slot_count, heads, depth)
    context = jnp.einsum(
        "shqk,skhd->sqhd", chances.astype(BF16), value_slots, preferred_element_type=F32
    )
    return (context.reshape(tokens, heads * depth), log_total)


def attention_backward(query, key, value, log_total, context_grad, lengths, slopes):
    tokens, heads, depth = query.shape
    slot_count = lengths.shape[0]
    span = tokens // slot_count
    scores = slot_scores(query, key, lengths, slopes)
    chances = jnp.exp(scores - log_total[..., None])
    output_slots = context_grad.reshape(slot_count, span, heads, depth)
    value_slots = value.reshape(slot_count, span, heads, depth)
    query_slots = query.reshape(slot_count, span, heads, depth)
    key_slots = key.reshape(slot_count, span, heads, depth)
    value_grad = jnp.einsum(
        "shqk,sqhd->skhd", chances.astype(BF16), output_slots, preferred_element_type=F32
    )
    chance_grad = jnp.einsum(
        "sqhd,skhd->shqk", output_slots, value_slots, preferred_element_type=F32
    )
    row_dot = jnp.sum(chances * chance_grad, axis=-1, keepdims=True)
    score_grad = (chances * (chance_grad - row_dot)).astype(BF16)
    factor = 1.0 / math.sqrt(depth)
    query_grad = (
        jnp.einsum("shqk,skhd->sqhd", score_grad, key_slots, preferred_element_type=F32) * factor
    )
    key_grad = (
        jnp.einsum("shqk,sqhd->skhd", score_grad, query_slots, preferred_element_type=F32) * factor
    )
    return (
        query_grad.reshape(tokens, heads, depth).astype(BF16),
        key_grad.reshape(tokens, heads, depth).astype(BF16),
        value_grad.reshape(tokens, heads, depth).astype(BF16),
    )


def shard_of(value):
    mean = lax.reduce_precision(jnp.mean(value, axis=1, keepdims=True), 8, 7)
    return packed((value - mean).astype(BF16), rows_of(mean), value.shape[1])


def weight_products(gain, shift, weight):
    def parts(v):
        high = lax.reduce_precision(v, 8, 7)
        return [high.astype(BF16), (v - high).astype(BF16)]

    rows = jnp.stack(parts(gain) + parts(shift))
    out = jnp.dot(rows, weight, preferred_element_type=F32)
    return out[0] + out[1], out[2] + out[3]


def sums_rows(first, second, width):
    extra = jnp.concatenate([rows_of(first), rows_of(second)], axis=0).astype(BF16)
    return jnp.pad(extra, ((0, PAD - extra.shape[0]), (0, width - extra.shape[1])))


def norm_backward(summed, centred, inverse, gain, width):
    tokens = centred.shape[0]
    groups = tokens // LANES
    gradient = summed[:tokens]
    first_sum = summed[tokens : tokens + groups, :LANES].reshape(tokens, 1)
    second_sum = summed[tokens + groups : tokens + 2 * groups, :LANES].reshape(tokens, 1)
    passed = inverse[:, :1] * (gradient * gain - first_sum / width - centred * (second_sum / width))
    return (passed, jnp.sum(gradient * centred, axis=0), jnp.sum(gradient, axis=0))


def on_device(
    activations,
    cotangent,
    lengths,
    first_gain,
    first_shift,
    joined_weight,
    query_bias,
    value_bias,
    output_weight,
    output_bias,
    second_gain,
    second_shift,
    up_weight,
    up_bias,
    down_weight,
    down_bias,
):
    tokens, f = activations.shape
    layers = first_gain.shape[0]
    blocks = 2 * ring_size()
    width = blocks * f
    heads_local = f // HEAD_DIM
    mine = block_index()

    smalls = (
        first_gain,
        first_shift,
        query_bias,
        value_bias,
        output_bias,
        second_gain,
        second_shift,
        down_bias,
    )
    table = jnp.concatenate([s.reshape(layers, 1, f) for s in smalls] + [up_bias.reshape(layers, -1, f)], axis=1)
    table = lax.all_gather(table, ("zh", "t"), axis=0)
    own_table = lax.dynamic_index_in_dim(table, mine, 0, keepdims=False)
    own_up = own_table[:, len(smalls) :].reshape(layers, -1)

    all_lengths = lax.all_gather(lengths, "c", axis=0)
    lengths = lax.dynamic_index_in_dim(all_lengths, lax.axis_index("zh"), 0, keepdims=False)

    head_index = mine * heads_local + jnp.arange(heads_local)
    slopes = jnp.exp2(-8.0 * (head_index + 1).astype(F32) / HEADS)
    slot_count = lengths.shape[0]
    span = tokens // slot_count
    valid = (jnp.arange(span)[None, :] < lengths[:, None]).reshape(tokens, 1)

    shard = swap_roles(shard_of(activations))
    residual = swap_roles(activations)
    no_rows = jnp.zeros((PAD, f), BF16)
    saved = []
    for layer in range(layers):
        joined_w = gather_weight(joined_weight[layer])
        output_w = gather_weight(output_weight[layer])
        up_w = gather_weight(up_weight[layer])
        down_w = gather_weight(down_weight[layer])
        joined_w = joined_w.reshape(width, -1)
        up_w = up_w.reshape(width, -1)
        gains = [table[:, layer, k] for k in range(len(smalls))]

        if layer > 0:
            shard = shard_of(residual)
        normed_one, centred_one, inverse_one = assemble_norm(
            gather_slots(shard), residual, gains[0], gains[1]
        )
        joined = jnp.dot(normed_one, joined_w, preferred_element_type=F32).reshape(
            tokens, heads_local, 3, HEAD_DIM
        )
        query_shift = own_table[layer, 2].reshape(heads_local, HEAD_DIM)
        value_shift = own_table[layer, 3].reshape(heads_local, HEAD_DIM)
        query = (joined[:, :, 0] + query_shift).astype(BF16)
        key = joined[:, :, 1].astype(BF16)
        value = (joined[:, :, 2] + value_shift).astype(BF16)
        context, log_total = attention_forward(query, key, value, lengths, slopes)
        context = context.astype(BF16)
        middle = (
            residual
            + column_sum(context, output_w, no_rows, False)[:tokens]
            + own_table[layer, 4]
        )
        normed_two, centred_two, inverse_two = assemble_norm(
            gather_slots(shard_of(middle)), middle, gains[5], gains[6]
        )
        upper = jnp.dot(normed_two, up_w, preferred_element_type=F32) + own_up[layer]
        activated = gelu_tanh(upper).astype(BF16)
        residual = (
            middle
            + column_sum(activated, down_w, no_rows, False)[:tokens]
            + own_table[layer, 7]
        )
        saved.append(
            (
                normed_one,
                centred_one,
                inverse_one,
                query,
                key,
                value,
                log_total,
                context,
                normed_two,
                centred_two,
                inverse_two,
                upper,
                activated,
                joined_w,
                output_w,
                up_w,
                down_w,
            )
        )
    result = swap_roles(residual)
    gradient = swap_roles(cotangent) * valid
    weight_terms = [None] * layers
    small_terms = [None] * layers
    passed_one = None
    for layer in reversed(range(layers)):
        (
            normed_one,
            centred_one,
            inverse_one,
            query,
            key,
            value,
            log_total,
            context,
            normed_two,
            centred_two,
            inverse_two,
            upper,
            activated,
            joined_w,
            output_w,
            up_w,
            down_w,
        ) = saved[layer]
        own = own_table[layer]
        gains = [table[:, layer, k].reshape(width) for k in range(len(smalls))]
        column_blocks = down_w.shape[0]

        down_bias_term = jnp.sum(gradient, axis=0)
        low_gradient = assemble(gather_slots(gradient.astype(BF16)))
        down_full = down_w.transpose(1, 0, 2).reshape(-1, width)
        hidden_grad = jnp.einsum("td,fd->tf", low_gradient, down_full, preferred_element_type=F32)
        upper_grad = jax.vjp(gelu_tanh, upper)[1](hidden_grad)[0].astype(BF16)
        wide_grad = upper_grad.astype(F32)
        gain_product, shift_product = weight_products(gains[5], gains[6], up_w)
        first_sum = jnp.sum(wide_grad * gain_product, axis=1)
        second_sum = jnp.sum(wide_grad * (upper - (own_up[layer] + shift_product)), axis=1)
        normed_two_grad = column_sum(upper_grad, up_w, sums_rows(first_sum, second_sum, f), True)
        up_bias_term = jnp.sum(wide_grad, axis=0)
        down_term = jnp.einsum("tf,td->fd", activated, low_gradient, preferred_element_type=F32)
        up_term = jnp.einsum("td,tf->df", normed_two, upper_grad, preferred_element_type=F32)
        passed_two, gain_two_term, shift_two_term = norm_backward(
            normed_two_grad, centred_two, inverse_two, own[5], width
        )
        middle_grad = gradient + passed_two
        output_bias_term = jnp.sum(middle_grad, axis=0)
        low_middle = assemble(gather_slots(middle_grad.astype(BF16)))
        output_full = output_w.transpose(1, 0, 2).reshape(-1, width)
        context_grad = jnp.einsum(
            "td,cd->tc", low_middle, output_full, preferred_element_type=F32
        ).astype(BF16)
        output_term = jnp.einsum("tc,td->cd", context, low_middle, preferred_element_type=F32)
        query_grad, key_grad, value_grad = attention_backward(
            query, key, value, log_total, context_grad, lengths, slopes
        )
        joined_grad = jnp.stack((query_grad, key_grad, value_grad), axis=2).reshape(tokens, 3 * f)
        query_shift = own[2].reshape(heads_local, HEAD_DIM)
        value_shift = own[3].reshape(heads_local, HEAD_DIM)
        joined_shift = jnp.stack(
            (query_shift, jnp.zeros_like(query_shift), value_shift), axis=1
        ).reshape(3 * f)
        joined = jnp.stack((query, key, value), axis=2).reshape(tokens, 3 * f)
        wide_grad = joined_grad.astype(F32)
        gain_product, shift_product = weight_products(gains[0], gains[1], joined_w)
        first_sum = jnp.sum(wide_grad * gain_product, axis=1)
        second_sum = jnp.sum(
            wide_grad * (joined.astype(F32) - (joined_shift + shift_product)), axis=1
        )
        normed_one_grad = column_sum(joined_grad, joined_w, sums_rows(first_sum, second_sum, f), True)
        query_bias_term = jnp.sum(query_grad.astype(F32), axis=0).reshape(f)
        value_bias_term = jnp.sum(value_grad.astype(F32), axis=0).reshape(f)
        joined_term = jnp.einsum("td,tc->dc", normed_one, joined_grad, preferred_element_type=F32)
        passed_one, gain_one_term, shift_one_term = norm_backward(
            normed_one_grad, centred_one, inverse_one, own[0], width
        )
        gradient = middle_grad + passed_one
        small_terms[layer] = jnp.concatenate(
            [
                t.reshape(-1, f)
                for t in (
                    gain_one_term,
                    shift_one_term,
                    query_bias_term,
                    value_bias_term,
                    output_bias_term,
                    gain_two_term,
                    shift_two_term,
                    down_bias_term,
                    up_bias_term,
                )
            ],
            axis=0,
        )

        def by_columns(term):
            return term.reshape(term.shape[0], column_blocks, -1).transpose(1, 0, 2)

        def by_rows(term):
            return term.reshape(column_blocks, -1, term.shape[1])

        weight_terms[layer] = (
            scatter_weight(by_rows(joined_term)),
            scatter_weight(by_columns(output_term)),
            scatter_weight(by_rows(up_term)),
            scatter_weight(by_columns(down_term)),
        )
    input_grad = swap_roles(middle_grad) + swap_roles(passed_one.astype(BF16)).astype(F32)
    small = lax.psum(jnp.stack(small_terms), ("rh", "zh"))
    same = lax.axis_index("c") == lax.axis_index("zh")
    small = jnp.where(same, small, partner(small))

    def weight_out(k):
        return jnp.stack([entry[k] for entry in weight_terms])

    return (
        result,
        input_grad,
        small[:, 0],
        small[:, 1],
        weight_out(0),
        small[:, 2],
        small[:, 3],
        weight_out(1),
        small[:, 4],
        small[:, 5],
        small[:, 6],
        weight_out(2),
        small[:, 8:].reshape(layers, -1),
        weight_out(3),
        small[:, 7],
    )


def solution(mesh):
    rows, columns = mesh.devices.shape
    inner = Mesh(mesh.devices.reshape(rows // 2, 2, 2, columns // 2), ("rh", "c", "zh", "t"))
    row, col = ("rh", "c"), ("zh", "t")
    return jax.shard_map(
        on_device,
        mesh=inner,
        in_specs=(
            P(row, col),
            P(row, col),
            P(row),
            P(None, col),
            P(None, col),
            P(None, row, col),
            P(None, col),
            P(None, col),
            P(None, col, row),
            P(None, col),
            P(None, col),
            P(None, col),
            P(None, row, col),
            P(None, col),
            P(None, col, row),
            P(None, col),
        ),
        out_specs=(
            P(row, col),
            P(row, col),
            P(None, col),
            P(None, col),
            P(None, row, col),
            P(None, col),
            P(None, col),
            P(None, col, row),
            P(None, col),
            P(None, col),
            P(None, col),
            P(None, row, col),
            P(None, col),
            P(None, col, row),
            P(None, col),
        ),
        check_vma=False,
    )
```

```python
import functools
import math

import jax
import jax.numpy as jnp
from jax import lax
from jax.experimental import pallas as pl
from jax.experimental.pallas import tpu as pltpu
from jax.sharding import Mesh
from jax.sharding import PartitionSpec as P

HEADS = 16
HEAD_DIM = 128
PAD = 16
LANES = 128
CHUNKS = 1
MIB = 2**20

norm_eps = 1e-05
masked_score = -1e30

F32 = jnp.float32
BF16 = jnp.bfloat16


def gelu_tanh(value):
    return jax.nn.gelu(value, approximate=True)


def after(value, *earlier):
    return lax.optimization_barrier((value, earlier))[0]


def ring_size():
    return lax.axis_size("t")


def ring(value, k):
    return lax.ppermute(value, "t", [(i, i ^ k) for i in range(ring_size())])


def partner(value):
    return lax.ppermute(value, "c", [(0, 1), (1, 0)])


def swap_roles(value):
    same = lax.axis_index("c") == lax.axis_index("x")
    return jnp.where(same, value, lax.ppermute(value, ("c", "x"), [(1, 2), (2, 1)]))


def block_index():
    return lax.axis_index("t") * 2 + lax.axis_index("c")


def slot_blocks():
    return (jnp.arange(2 * ring_size(), dtype=jnp.int32) ^ block_index()).astype(jnp.int32)


def gather_slots(value):
    if ring_size() == 4:
        far = ring(value, 2)
        mine = [value, ring(value, 1), far, ring(far, 1)]
    else:
        mine = [value] + [ring(value, k) for k in range(1, ring_size())]
    return [v for m in mine for v in (m, partner(m))]


def pair_blocks(mine, other):
    got = partner(other)
    pair = mine.astype(F32) + got.astype(F32)
    return [pair[0]] + [pair[k].astype(BF16) for k in range(1, ring_size())]


def ring_sum(pair):
    if ring_size() == 4:
        far = pair[2].astype(F32) + ring(pair[3], 1).astype(F32)
        got = [ring(pair[1], 1), ring(far.astype(BF16), 2)]
    else:
        got = [ring(pair[k], k) for k in range(1, ring_size())]
    return added([pair[0]] + [g.astype(F32) for g in got])


def whole(shape):
    return pl.BlockSpec(shape, lambda *_: (0,) * len(shape))


def assemble_norm_kernel(slots, width, blocks_ref, *refs):
    shards = refs[:slots]
    means_ref, spread_ref, gain_ref, shift_ref, own_ref = refs[slots : slots + 5]
    out_ref, centred_ref, inverse_ref = refs[slots + 5 :]
    f = shards[0].shape[1]
    offsets = lax.dot_general(
        means_ref[0].astype(BF16),
        spread_ref[...],
        (((0,), (0,)), ((), ())),
        preferred_element_type=F32,
    )
    values = [shards[s][...].astype(F32) + offsets[:, s * f : (s + 1) * f] for s in range(slots)]
    total = values[0]
    for v in values[1:]:
        total = total + v
    mean = jnp.sum(total, axis=1, keepdims=True) / width
    values = [v - mean for v in values]
    squares = values[0] * values[0]
    for v in values[1:]:
        squares = squares + v * v
    inverse = lax.rsqrt(jnp.sum(squares, axis=1, keepdims=True) / width + norm_eps)
    for s in range(slots):
        block = blocks_ref[s]
        normed = values[s] * inverse * gain_ref[s] + shift_ref[s]
        out_ref[:, pl.ds(pl.multiple_of(block * f, f), f)] = normed.astype(BF16)
    centred_ref[...] = (own_ref[...] - mean) * inverse
    inverse_ref[...] = jnp.broadcast_to(inverse, inverse_ref.shape)


def assemble_norm(shards, own, gain, shift):
    slots = len(shards)
    tokens, f = own.shape
    width = slots * f
    groups = tokens // LANES
    means = jnp.stack([s[tokens : tokens + groups, :LANES] for s in shards], axis=1).astype(F32)
    spread = jnp.repeat(jnp.eye(slots, dtype=BF16), f, axis=1)
    tile = LANES
    return pl.pallas_call(
        functools.partial(assemble_norm_kernel, slots, width),
        grid_spec=pltpu.PrefetchScalarGridSpec(
            num_scalar_prefetch=1,
            grid=(tokens // tile,),
            in_specs=[pl.BlockSpec((tile, f), lambda g, b: (g, 0))] * slots
            + [
                pl.BlockSpec((1, slots, LANES), lambda g, b: (g, 0, 0)),
                whole((slots, width)),
                whole((slots, 1, f)),
                whole((slots, 1, f)),
                pl.BlockSpec((tile, f), lambda g, b: (g, 0)),
            ],
            out_specs=[
                pl.BlockSpec((tile, width), lambda g, b: (g, 0)),
                pl.BlockSpec((tile, f), lambda g, b: (g, 0)),
                pl.BlockSpec((tile, LANES), lambda g, b: (g, 0)),
            ],
        ),
        out_shape=[
            jax.ShapeDtypeStruct((tokens, width), BF16),
            jax.ShapeDtypeStruct((tokens, f), F32),
            jax.ShapeDtypeStruct((tokens, LANES), F32),
        ],
        compiler_params=pltpu.CompilerParams(vmem_limit_bytes=24 * MIB),
        cost_estimate=pl.CostEstimate(
            flops=12 * tokens * width, bytes_accessed=6 * tokens * width, transcendentals=tokens
        ),
        name="assemble_norm",
    )(
        slot_blocks(),
        *shards,
        means,
        spread,
        gain.reshape(slots, 1, f),
        shift.reshape(slots, 1, f),
        own,
    )


def assemble_kernel(slots, blocks_ref, *refs):
    out_ref = refs[slots]
    f = refs[0].shape[1]
    for s in range(slots):
        out_ref[:, pl.ds(pl.multiple_of(blocks_ref[s] * f, f), f)] = refs[s][...]


def assemble(shards):
    slots = len(shards)
    tokens, f = shards[0].shape
    tile = min(tokens, 256)
    return pl.pallas_call(
        functools.partial(assemble_kernel, slots),
        grid_spec=pltpu.PrefetchScalarGridSpec(
            num_scalar_prefetch=1,
            grid=(tokens // tile,),
            in_specs=[pl.BlockSpec((tile, f), lambda g, b: (g, 0))] * slots,
            out_specs=pl.BlockSpec((tile, slots * f), lambda g, b: (g, 0)),
        ),
        out_shape=jax.ShapeDtypeStruct((tokens, slots * f), BF16),
        compiler_params=pltpu.CompilerParams(vmem_limit_bytes=24 * MIB),
        cost_estimate=pl.CostEstimate(
            flops=0, bytes_accessed=4 * tokens * slots * f, transcendentals=0
        ),
        name="assemble",
    )(slot_blocks(), *shards)


def pack_kernel(turned, *refs):
    out_ref = refs[-1]
    at = 0
    for turn, ref in zip(turned, refs):
        value = ref[0].T if turn else ref[0]
        out_ref[:, at : at + value.shape[1]] = value.astype(BF16)
        at += value.shape[1]


def pack(blocks, turned, layer):
    tile = LANES
    rows = blocks[0].shape[2 if turned[0] else 1]
    counts = [b.shape[1 if t else 2] for b, t in zip(blocks, turned)]
    return pl.pallas_call(
        functools.partial(pack_kernel, turned),
        grid=(rows // tile,),
        in_specs=[
            pl.BlockSpec((1, n, tile), lambda g: (layer, 0, g))
            if t
            else pl.BlockSpec((1, tile, n), lambda g: (layer, g, 0))
            for n, t in zip(counts, turned)
        ],
        out_specs=pl.BlockSpec((tile, sum(counts)), lambda g: (g, 0)),
        out_shape=jax.ShapeDtypeStruct((rows, sum(counts)), BF16),
        compiler_params=pltpu.CompilerParams(vmem_limit_bytes=24 * MIB),
        cost_estimate=pl.CostEstimate(
            flops=0, bytes_accessed=6 * rows * sum(counts), transcendentals=0
        ),
        name="pack",
    )(*blocks)


def unpack_kernel(layers, turned, counts, same_ref, *refs):
    outs = refs[2 * layers :]
    for layer in range(layers):

        @pl.when(pl.program_id(0) == layer)
        def _():
            own, received = refs[2 * layer][...].astype(F32), refs[2 * layer + 1][...].astype(F32)
            value = jnp.where(same_ref[0] == 1, own, received)
            at = 0
            for turn, count, out in zip(turned, counts, outs):
                piece = value[:, at : at + count]
                out[0] = piece.T if turn else piece
                at += count


def unpack(pairs, turned, counts):
    layers = len(pairs)
    rows, columns = pairs[0][0].shape
    tile = LANES
    same = (lax.axis_index("c") == lax.axis_index("x")).astype(jnp.int32).reshape(1)
    return pl.pallas_call(
        functools.partial(unpack_kernel, layers, turned, counts),
        grid_spec=pltpu.PrefetchScalarGridSpec(
            num_scalar_prefetch=1,
            grid=(layers, rows // tile),
            in_specs=[
                pl.BlockSpec((tile, columns), lambda n, g, _, layer=layer: (jnp.where(n == layer, g, 0), 0))
                for layer in range(layers)
                for _ in range(2)
            ],
            out_specs=[
                pl.BlockSpec((1, n, tile), lambda n, g, _: (n, 0, g))
                if t
                else pl.BlockSpec((1, tile, n), lambda n, g, _: (n, g, 0))
                for n, t in zip(counts, turned)
            ],
        ),
        out_shape=[
            jax.ShapeDtypeStruct((layers, n, rows) if t else (layers, rows, n), F32)
            for n, t in zip(counts, turned)
        ],
        compiler_params=pltpu.CompilerParams(vmem_limit_bytes=24 * MIB),
        cost_estimate=pl.CostEstimate(
            flops=0, bytes_accessed=8 * layers * rows * columns, transcendentals=0
        ),
        name="unpack",
    )(same, *[v for pair in pairs for v in pair])


def slot_matmul_kernel(tile, blocks_ref, x_ref, w_ref, extra_ref, out_ref):
    tokens = x_ref.shape[0]
    for g in range(tokens // tile):
        at = pl.ds(g * tile, tile)
        out_ref[0, at, :] = lax.dot_general(
            x_ref[at, :], w_ref[...], (((1,), (1,)), ((), ())), preferred_element_type=F32
        ).astype(BF16)
    out_ref[0, tokens:, :] = extra_ref[...]


def slot_matmul(x, w, extra, other):
    tokens, depth = x.shape
    n = ring_size()
    f = extra.shape[1]
    blocks = slot_blocks()[1 if other else 0 :: 2]
    tile = min(tokens, 512)
    return pl.pallas_call(
        functools.partial(slot_matmul_kernel, tile),
        grid_spec=pltpu.PrefetchScalarGridSpec(
            num_scalar_prefetch=1,
            grid=(n,),
            in_specs=[
                whole((tokens, depth)),
                pl.BlockSpec((f, depth), lambda k, b: (b[k], 0)),
                whole((PAD, f)),
            ],
            out_specs=pl.BlockSpec((1, tokens + PAD, f), lambda k, b: (k, 0, 0)),
        ),
        out_shape=jax.ShapeDtypeStruct((n, tokens + PAD, f), BF16),
        compiler_params=pltpu.CompilerParams(vmem_limit_bytes=24 * MIB),
        cost_estimate=pl.CostEstimate(
            flops=2 * tokens * depth * n * f,
            bytes_accessed=2 * (tokens * depth + n * f * (depth + tokens)),
            transcendentals=0,
        ),
        name="slot_matmul",
    )(blocks, x, w, extra)


def column_sum(x, w, extra):
    other = slot_matmul(x, w, extra, True)
    mine = slot_matmul(x, w, extra, False)
    return pair_blocks(mine, other)


def block_scores(query, key, row0, column0, length, slope):
    rows, columns = query.shape[0], key.shape[0]
    scores = lax.dot_general(
        query, key, (((1,), (1,)), ((), ())), preferred_element_type=F32
    ) * (1.0 / math.sqrt(HEAD_DIM))
    row = lax.broadcasted_iota(jnp.int32, (rows, columns), 0) + row0
    column = lax.broadcasted_iota(jnp.int32, (rows, columns), 1) + column0
    scores = scores - slope * (row - column).astype(F32)
    return jnp.where((column <= row) & (column < length), scores, masked_score)


def attend_kernel(chunk, tile, length_ref, slope_ref, q_ref, *refs):
    keys, values = refs[: chunk + 1], refs[chunk + 1 : 2 * chunk + 2]
    context_ref, log_ref = refs[2 * chunk + 2 :]
    h, g = pl.program_id(0), pl.program_id(1)
    span = keys[0].shape[0]
    query = q_ref[...]
    scores = [
        block_scores(query, keys[m][...], chunk * span + g * tile, m * span, length_ref[0], slope_ref[h])
        for m in range(chunk + 1)
    ]
    highest = functools.reduce(jnp.maximum, [jnp.max(s, axis=1, keepdims=True) for s in scores])
    raised = [jnp.exp(s - highest) for s in scores]
    total = sum(jnp.sum(r, axis=1, keepdims=True) for r in raised)
    context = sum(
        jnp.dot((r / total).astype(BF16), v[...], preferred_element_type=F32)
        for r, v in zip(raised, values)
    )
    context_ref[...] = context.astype(BF16)
    log_ref[...] = jnp.broadcast_to(highest + jnp.log(total), log_ref.shape)


def attend(chunk, joined, length, slopes):
    span, columns = joined[0].shape
    heads = columns // (3 * HEAD_DIM)
    tile = min(span, 256)
    own = joined[chunk]
    return pl.pallas_call(
        functools.partial(attend_kernel, chunk, tile),
        grid_spec=pltpu.PrefetchScalarGridSpec(
            num_scalar_prefetch=2,
            grid=(heads, span // tile),
            in_specs=[pl.BlockSpec((tile, HEAD_DIM), lambda h, g, *_: (g, 3 * h))]
            + [pl.BlockSpec((span, HEAD_DIM), lambda h, g, *_: (0, 3 * h + 1))] * (chunk + 1)
            + [pl.BlockSpec((span, HEAD_DIM), lambda h, g, *_: (0, 3 * h + 2))] * (chunk + 1),
            out_specs=[pl.BlockSpec((tile, HEAD_DIM), lambda h, g, *_: (g, h))] * 2,
        ),
        out_shape=[
            jax.ShapeDtypeStruct((span, heads * HEAD_DIM), BF16),
            jax.ShapeDtypeStruct((span, heads * HEAD_DIM), F32),
        ],
        compiler_params=pltpu.CompilerParams(vmem_limit_bytes=32 * MIB),
        cost_estimate=pl.CostEstimate(
            flops=4 * span * span * (chunk + 1) * heads * HEAD_DIM,
            bytes_accessed=8 * span * columns * (chunk + 1),
            transcendentals=span * span * (chunk + 1) * heads,
        ),
        name="attend",
    )(length, slopes, own, *joined[: chunk + 1], *joined[: chunk + 1])


def attend_back_kernel(chunk, last, tile, length_ref, slope_ref, q_ref, *refs):
    n = chunk + 1
    keys, values, refs = refs[:n], refs[n : 2 * n], refs[2 * n :]
    given = []
    if not last:
        given, refs = refs[:n], refs[n:]
    grad_ref, log_ref, refs = refs[0], refs[1], refs[2:]
    out_ref, sums, refs = refs[0], refs[1:n], refs[n:]
    key_sums, value_sums = refs[:n], refs[n:]
    h, g = pl.program_id(0), pl.program_id(1)
    span = keys[0].shape[0]
    d = HEAD_DIM

    @pl.when(g == 0)
    def _():
        for m in range(n):
            if last:
                key_sums[m][...] = jnp.zeros((span, d), F32)
                value_sums[m][...] = jnp.zeros((span, d), F32)
            else:
                key_sums[m][...] = given[m][:, :d]
                value_sums[m][...] = given[m][:, d:]

    query, grad = q_ref[...], grad_ref[...]
    log_total = log_ref[:, :1]
    by_rows = (((0,), (0,)), ((), ()))
    chances, chance_grads = [], []
    for m in range(n):
        scores = block_scores(
            query, keys[m][...], chunk * span + g * tile, m * span, length_ref[0], slope_ref[h]
        )
        chances.append(jnp.exp(scores - log_total))
        chance_grads.append(
            lax.dot_general(grad, values[m][...], (((1,), (1,)), ((), ())), preferred_element_type=F32)
        )
    row_dot = sum(
        jnp.sum(p * c, axis=1, keepdims=True) for p, c in zip(chances, chance_grads)
    )
    query_grad = jnp.zeros((tile, d), F32)
    for m in range(n):
        value_sums[m][...] += lax.dot_general(
            chances[m].astype(BF16), grad, by_rows, preferred_element_type=F32
        )
        score_grad = (chances[m] * (chance_grads[m] - row_dot)).astype(BF16)
        query_grad += jnp.dot(score_grad, keys[m][...], preferred_element_type=F32)
        key_sums[m][...] += lax.dot_general(
            score_grad, query, by_rows, preferred_element_type=F32
        )
    factor = 1.0 / math.sqrt(d)
    out_ref[pl.ds(pl.multiple_of(g * tile, tile), tile), :d] = (query_grad * factor).astype(BF16)

    @pl.when(g == pl.num_programs(1) - 1)
    def _():
        out_ref[:, d : 2 * d] = (key_sums[chunk][...] * factor).astype(BF16)
        out_ref[:, 2 * d :] = value_sums[chunk][...].astype(BF16)
        for m in range(chunk):
            sums[m][:, :d] = key_sums[m][...]
            sums[m][:, d:] = value_sums[m][...]


def attend_back(chunk, joined, given, context_grad, log_total, length, slopes):
    span, columns = joined[0].shape
    heads = columns // (3 * HEAD_DIM)
    tile = min(span, 256)
    n = chunk + 1
    last = given is None
    wide = pl.BlockSpec((span, 2 * HEAD_DIM), lambda h, g, *_: (0, h))
    tall = pl.BlockSpec((tile, HEAD_DIM), lambda h, g, *_: (g, h))
    outs = pl.pallas_call(
        functools.partial(attend_back_kernel, chunk, last, tile),
        grid_spec=pltpu.PrefetchScalarGridSpec(
            num_scalar_prefetch=2,
            grid=(heads, span // tile),
            in_specs=[pl.BlockSpec((tile, HEAD_DIM), lambda h, g, *_: (g, 3 * h))]
            + [pl.BlockSpec((span, HEAD_DIM), lambda h, g, *_: (0, 3 * h + 1))] * n
            + [pl.BlockSpec((span, HEAD_DIM), lambda h, g, *_: (0, 3 * h + 2))] * n
            + [wide] * (0 if last else n)
            + [tall, tall],
            out_specs=[pl.BlockSpec((span, 3 * HEAD_DIM), lambda h, g, *_: (0, h))] + [wide] * chunk,
            scratch_shapes=[pltpu.VMEM((span, HEAD_DIM), F32)] * (2 * n),
        ),
        out_shape=[jax.ShapeDtypeStruct((span, columns), BF16)]
        + [jax.ShapeDtypeStruct((span, heads * 2 * HEAD_DIM), F32)] * chunk,
        compiler_params=pltpu.CompilerParams(vmem_limit_bytes=40 * MIB),
        cost_estimate=pl.CostEstimate(
            flops=10 * span * span * n * heads * HEAD_DIM,
            bytes_accessed=12 * span * columns * n,
            transcendentals=span * span * n * heads,
        ),
        name="attend_back",
    )(
        length,
        slopes,
        joined[chunk],
        *joined[:n],
        *joined[:n],
        *([] if last else given),
        context_grad,
        log_total,
    )
    return outs[0], list(outs[1:])


def rows_of(column):
    return column.reshape(-1, LANES)


def packed(value, rows, width):
    extra = jnp.pad(rows.astype(value.dtype), ((0, PAD - rows.shape[0]), (0, width - rows.shape[1])))
    return jnp.concatenate([value, extra], axis=0)


def shard_of(value):
    mean = lax.reduce_precision(jnp.mean(value, axis=1, keepdims=True), 8, 7)
    return packed((value - mean).astype(BF16), rows_of(mean), value.shape[1])


def weight_products(gain, shift, weight):
    def parts(v):
        high = lax.reduce_precision(v, 8, 7)
        return [high.astype(BF16), (v - high).astype(BF16)]

    rows = jnp.stack(parts(gain) + parts(shift))
    out = jnp.dot(rows, weight, preferred_element_type=F32)
    return out[0] + out[1], out[2] + out[3]


def sums_rows(first, second, width):
    extra = jnp.concatenate([rows_of(first), rows_of(second)], axis=0).astype(BF16)
    return jnp.pad(extra, ((0, PAD - extra.shape[0]), (0, width - extra.shape[1])))


def norm_backward(summed, centred, inverse, gain, width):
    tokens = centred.shape[0]
    groups = tokens // LANES
    gradient = summed[:tokens]
    first_sum = summed[tokens : tokens + groups, :LANES].reshape(tokens, 1)
    second_sum = summed[tokens + groups : tokens + 2 * groups, :LANES].reshape(tokens, 1)
    passed = inverse[:, :1] * (gradient * gain - first_sum / width - centred * (second_sum / width))
    return (passed, jnp.sum(gradient * centred, axis=0), jnp.sum(gradient, axis=0))


def added(items):
    return functools.reduce(jnp.add, items)


def three_parts(value):
    terms = []
    for _ in range(3):
        high = lax.reduce_precision(value, 8, 7)
        terms.append(high.astype(BF16))
        value = value - high
    return terms


def gather_weight(block):
    return lax.all_gather(block, ("rh", "c", "x"), axis=0, tiled=True)


def own_columns(blocks, rows):
    n = blocks.shape[1]
    blocks = blocks.reshape(-1, 2, rows, n)
    return lax.dynamic_index_in_dim(blocks, lax.axis_index("c"), 1, keepdims=False).reshape(-1, n)


def scatter_weight(term):
    return lax.psum_scatter(term, ("rh", "x"), scatter_dimension=0, tiled=True)


def swapped(value):
    return value, lax.ppermute(value, ("c", "x"), [(1, 2), (2, 1)])


def on_device(
    activations,
    cotangent,
    lengths,
    first_gain,
    first_shift,
    joined_weight,
    query_bias,
    value_bias,
    output_weight,
    output_bias,
    second_gain,
    second_shift,
    up_weight,
    up_bias,
    down_weight,
    down_bias,
):
    tokens, f = activations.shape
    layers = first_gain.shape[0]
    width = 2 * ring_size() * f
    heads_local = f // HEAD_DIM
    span = tokens // CHUNKS
    chunks = range(CHUNKS)

    def cut(value):
        return [value[k * span : (k + 1) * span] for k in chunks]

    lengths = swap_roles(lengths)
    head_index = block_index() * heads_local + jnp.arange(heads_local)
    slopes = jnp.exp2(-8.0 * (head_index + 1).astype(F32) / HEADS)
    valid = (jnp.arange(tokens) < lengths[0]).reshape(tokens, 1)

    smalls = (
        first_gain,
        first_shift,
        query_bias,
        value_bias,
        output_bias,
        second_gain,
        second_shift,
        down_bias,
    )
    table = jnp.concatenate(
        [s.reshape(layers, 1, f) for s in smalls] + [up_bias.reshape(layers, -1, f)], axis=1
    )
    table_rows = table.shape[1]
    count = layers * table_rows
    table = jnp.concatenate(three_parts(table.reshape(count, f)), axis=0)
    table = jnp.pad(table, ((0, -table.shape[0] % PAD), (0, 0)))
    shards = [shard_of(v) for v in cut(activations)]
    shards[0] = jnp.concatenate([shards[0], table], axis=0)
    shards = [swap_roles(s) for s in shards]
    residual = [swap_roles(after(v, *shards)) for v in cut(activations)]

    packs = []
    for layer in range(layers):
        blocks = (
            pack((joined_weight, output_weight), (False, True), layer),
            pack((up_weight,), (False,), layer),
            pack((down_weight,), (True,), layer),
        )
        if layer == 0:
            blocks, _ = lax.optimization_barrier((blocks, shards))
        packs.append([gather_weight(b) for b in blocks])
        if layer == 0:
            gradient = [swap_roles(after(v, packs[0][0])) * m for v, m in zip(cut(cotangent), cut(valid))]
    rows = joined_weight.shape[1]
    weights = []

    slots = [gather_slots(s) for s in shards]
    held = jnp.stack([s[span + PAD :][: 3 * count] for s in slots[0]]).astype(F32)
    table = (held[:, :count] + held[:, count : 2 * count] + held[:, 2 * count :]).reshape(
        len(slots[0]), layers, table_rows, f
    )
    own_up = table[0, :, len(smalls) :].reshape(layers, -1)

    no_rows = jnp.zeros((PAD, f), BF16)
    saved = []
    first_slots = [None] * CHUNKS
    turn = ()
    for layer in range(layers):
        last = layer + 1 == layers
        first_w = own_columns(packs[layer][0], rows)
        joined_w, output_w = first_w[:, : 3 * f], first_w[:, 3 * f :]
        gains = [table[:, layer, n] for n in range(len(smalls))]
        own = table[0, layer]
        zero = jnp.zeros((heads_local, HEAD_DIM), F32)
        joined_bias = jnp.stack(
            (own[2].reshape(heads_local, HEAD_DIM), zero, own[3].reshape(heads_local, HEAD_DIM)), axis=1
        ).reshape(3 * f)
        joined, kept = [], []
        for k in chunks:
            if layer > 0:
                slots[k] = gather_slots(shard_of(residual[k]))
            slots[k], _ = lax.optimization_barrier((slots[k], turn))
            normed_one, centred_one, inverse_one = assemble_norm(
                slots[k], residual[k], gains[0], gains[1]
            )
            joined.append(
                (jnp.dot(normed_one, joined_w, preferred_element_type=F32) + joined_bias).astype(BF16)
            )
            if last:
                first_slots[k] = gather_slots(after(gradient[k].astype(BF16), normed_one))
            context, log_total = attend(k, joined, lengths, slopes)
            if last:
                context = after(context, *first_slots[k])
            pair = column_sum(context, output_w, no_rows)
            turn = pair
            middle = residual[k] + ring_sum(pair)[:span] + own[4]
            kept.append([normed_one, centred_one, inverse_one, context, log_total, middle])
        up_w = own_columns(after(packs[layer][1], turn), rows)
        for k in chunks:
            middle = kept[k].pop()
            slots[k] = gather_slots(shard_of(middle))
            slots[k], _ = lax.optimization_barrier((slots[k], turn))
            normed_two, centred_two, inverse_two = assemble_norm(slots[k], middle, gains[5], gains[6])
            upper = jnp.dot(normed_two, up_w, preferred_element_type=F32) + own_up[layer]
            activated = gelu_tanh(upper).astype(BF16)
            if k == 0:
                down_w = own_columns(after(packs[layer][2], upper), rows)
            turn = (activated,)
            if not last:
                pair = column_sum(activated, down_w, no_rows)
                turn = pair
                residual[k] = middle + ring_sum(pair)[:span] + own[7]
            kept[k] += [normed_two, centred_two, inverse_two, upper, activated, middle]
        weights.append((joined_w, output_w, up_w, down_w))
        saved.append((joined, joined_bias, kept))

    weight_terms = [None] * layers
    small_terms = [None] * layers
    result = [None] * CHUNKS
    middle_grad = [None] * CHUNKS
    passed_one = [None] * CHUNKS

    def term(pieces):
        return added(
            [jnp.einsum("td,tn->dn", a, b, preferred_element_type=F32) for a, b in pieces]
        ).astype(BF16)

    for layer in reversed(range(layers)):
        joined, joined_bias, kept = saved[layer]
        joined_w, output_w, up_w, down_w = weights[layer]
        own = table[0, layer]
        order = slot_blocks()
        gains = [table[order, layer, n].reshape(width) for n in range(len(smalls))]
        up_gain, up_shift = weight_products(gains[5], gains[6], up_w)
        joined_gain, joined_shift = weight_products(gains[0], gains[1], joined_w)
        given = None
        smalls_of, down_ends, up_ends, joined_ends, output_ends = ([None] * CHUNKS for _ in range(5))
        for k in reversed(chunks):
            normed_two, centred_two, inverse_two, upper, activated, middle = kept[k][5:]
            down_bias_term = jnp.sum(gradient[k], axis=0)
            slots = first_slots[k] if layer + 1 == layers else gather_slots(gradient[k].astype(BF16))
            slots, _ = lax.optimization_barrier((slots, turn))
            low_gradient = assemble(slots)
            hidden_grad = jnp.dot(low_gradient, down_w, preferred_element_type=F32)
            upper_grad = jax.vjp(gelu_tanh, upper)[1](hidden_grad)[0].astype(BF16)
            wide_grad = upper_grad.astype(F32)
            first_sum = jnp.sum(wide_grad * up_gain, axis=1)
            second_sum = jnp.sum(wide_grad * (upper - (own_up[layer] + up_shift)), axis=1)
            up_bias_term = jnp.sum(wide_grad, axis=0)
            pair = column_sum(upper_grad, up_w, sums_rows(first_sum, second_sum, f))
            turn = pair
            down_ends[k] = (low_gradient, after(activated, pair))
            normed_two_grad = ring_sum(pair)
            if k == 0:
                down_term = term(down_ends)
                normed_two_grad = after(normed_two_grad, down_term)
                if layer + 1 < layers:
                    normed_two_grad = after(normed_two_grad, joint_sum)
                down_sum = scatter_weight(down_term)
            passed_two, gain_two_term, shift_two_term = norm_backward(
                normed_two_grad, centred_two, inverse_two, own[5], width
            )
            middle_grad[k] = gradient[k] + passed_two
            output_bias_term = jnp.sum(middle_grad[k], axis=0)
            smalls_of[k] = [output_bias_term, gain_two_term, shift_two_term, down_bias_term, up_bias_term]
            up_ends[k] = (normed_two, after(upper_grad, middle_grad[k]))
        for k in reversed(chunks):
            normed_one, centred_one, inverse_one, context, log_total = kept[k][:5]
            activated, middle = kept[k][9:]
            slots = gather_slots(middle_grad[k].astype(BF16))
            slots, _ = lax.optimization_barrier((slots, turn))
            if k == 0:
                up_term = term(up_ends)
                slots, _ = lax.optimization_barrier((slots, (up_term, down_sum)))
                up_sum = scatter_weight(up_term)
            low_middle = assemble(slots)
            context_grad = jnp.dot(low_middle, output_w, preferred_element_type=F32).astype(BF16)
            if layer + 1 == layers:
                last_pair = column_sum(after(activated, context_grad), down_w, no_rows)
                result[k] = middle + ring_sum(last_pair)[:span] + own[7]
            joined_grad, given = attend_back(
                k, joined, given, context_grad, log_total, lengths, slopes
            )
            if layer + 1 == layers:
                joined_grad, result[k] = lax.optimization_barrier((joined_grad, result[k]))
            wide_grad = joined_grad.astype(F32)
            first_sum = jnp.sum(wide_grad * joined_gain, axis=1)
            second_sum = jnp.sum(
                wide_grad * (joined[k].astype(F32) - (joined_bias + joined_shift)), axis=1
            )
            joined_ends[k] = (normed_one, joined_grad)
            output_ends[k] = (low_middle, context)
            if k == 0 and layer == 0:
                first_term = jnp.concatenate([term(joined_ends), term(output_ends)], axis=1)
                first_sum = after(first_sum, first_term)
            pair = column_sum(joined_grad, joined_w, sums_rows(first_sum, second_sum, f))
            turn = pair
            normed_one_grad = ring_sum(pair)
            if k == 0 and layer > 0:
                joined_ends[0] = (normed_one, after(joined_grad, pair))
                output_ends[0] = (low_middle, after(context, pair))
                first_term = jnp.concatenate([term(joined_ends), term(output_ends)], axis=1)
                normed_one_grad = after(normed_one_grad, first_term, up_sum)
            if k == 0:
                joint_sum = scatter_weight(first_term)
            joined_bias_term = jnp.sum(joined_grad.astype(F32), axis=0).reshape(heads_local, 3, HEAD_DIM)
            passed_one[k], gain_one_term, shift_one_term = norm_backward(
                normed_one_grad, centred_one, inverse_one, own[0], width
            )
            gradient[k] = middle_grad[k] + passed_one[k]
            smalls_of[k] = jnp.concatenate(
                [
                    t.reshape(-1, f)
                    for t in (
                        gain_one_term,
                        shift_one_term,
                        joined_bias_term[:, 0],
                        joined_bias_term[:, 2],
                        *smalls_of[k],
                    )
                ],
                axis=0,
            )
        small_terms[layer] = added(smalls_of)
        weight_terms[layer] = [swapped(v) for v in (joint_sum, up_sum, down_sum)]
    input_grad = jnp.concatenate(
        [swap_roles(m) + swap_roles(p.astype(BF16)).astype(F32) for m, p in zip(middle_grad, passed_one)],
        axis=0,
    )
    small = jnp.stack(small_terms)
    for axis in ("rh", "x"):
        size = lax.axis_size(axis)
        small = small + added(
            [lax.ppermute(small, axis, [(r, r ^ k) for r in range(size)]) for k in range(1, size)]
        )
    same = lax.axis_index("c") == lax.axis_index("x")
    small = jnp.where(same, small, partner(small))

    joined_out, output_out = unpack([t[0] for t in weight_terms], (False, True), (3 * f, f))
    (up_out,) = unpack([t[1] for t in weight_terms], (False,), (up_weight.shape[2],))
    (down_out,) = unpack([t[2] for t in weight_terms], (True,), (down_weight.shape[1],))

    return (
        jnp.concatenate([swap_roles(r) for r in result], axis=0),
        input_grad,
        small[:, 0],
        small[:, 1],
        joined_out,
        small[:, 2],
        small[:, 3],
        output_out,
        small[:, 4],
        small[:, 5],
        small[:, 6],
        up_out,
        small[:, 8:].reshape(layers, -1),
        down_out,
        small[:, 7],
    )


def solution(mesh):
    rows, columns = mesh.devices.shape
    inner = Mesh(mesh.devices.reshape(rows // 2, 2, columns // 2, 2), ("rh", "c", "t", "x"))
    row, col = ("rh", "c"), ("t", "x")
    return jax.shard_map(
        on_device,
        mesh=inner,
        in_specs=(
            P(row, col),
            P(row, col),
            P(row),
            P(None, col),
            P(None, col),
            P(None, row, col),
            P(None, col),
            P(None, col),
            P(None, col, row),
            P(None, col),
            P(None, col),
            P(None, col),
            P(None, row, col),
            P(None, col),
            P(None, col, row),
            P(None, col),
        ),
        out_specs=(
            P(row, col),
            P(row, col),
            P(None, col),
            P(None, col),
            P(None, row, col),
            P(None, col),
            P(None, col),
            P(None, col, row),
            P(None, col),
            P(None, col),
            P(None, col),
            P(None, row, col),
            P(None, col),
            P(None, col, row),
            P(None, col),
        ),
        check_vma=False,
    )
```

```python
import functools
import math

import jax
import jax.numpy as jnp
from jax import lax
from jax.experimental import pallas as pl
from jax.experimental.pallas import tpu as pltpu
from jax.sharding import Mesh
from jax.sharding import PartitionSpec as P

HEADS = 16
HEAD_DIM = 128
PAD = 16
LANES = 128
CHUNKS = 1
MIB = 2**20
SCALE = 0.25


def cost(flops, bytes_accessed, transcendentals):
    return pl.CostEstimate(
        flops=int(flops * SCALE),
        bytes_accessed=int(bytes_accessed * SCALE),
        transcendentals=int(transcendentals * SCALE),
    )

norm_eps = 1e-05
masked_score = -1e30

F32 = jnp.float32
BF16 = jnp.bfloat16


def gelu_tanh(value):
    return jax.nn.gelu(value, approximate=True)


def after(value, *earlier):
    return lax.optimization_barrier((value, earlier))[0]


def ring_size():
    return lax.axis_size("t")


def ring(value, k):
    return lax.ppermute(value, "t", [(i, i ^ k) for i in range(ring_size())])


def partner(value):
    return lax.ppermute(value, "c", [(0, 1), (1, 0)])


def swap_roles(value):
    same = lax.axis_index("c") == lax.axis_index("x")
    return jnp.where(same, value, lax.ppermute(value, ("c", "x"), [(1, 2), (2, 1)]))


def block_index():
    return lax.axis_index("t") * 2 + lax.axis_index("c")


def slot_blocks():
    return (jnp.arange(2 * ring_size(), dtype=jnp.int32) ^ block_index()).astype(jnp.int32)


def gather_slots(value):
    if ring_size() == 4:
        far = ring(value, 2)
        mine = [value, ring(value, 1), far, ring(far, 1)]
    else:
        mine = [value] + [ring(value, k) for k in range(1, ring_size())]
    return [v for m in mine for v in (m, partner(m))]


def pair_blocks(mine, other):
    pair = [m.astype(F32) + partner(o).astype(F32) for m, o in zip(mine, other)]
    return [pair[0]] + [p.astype(BF16) for p in pair[1:]]


def ring_sum(pair):
    if ring_size() == 4:
        far = pair[2].astype(F32) + ring(pair[3], 1).astype(F32)
        got = [ring(pair[1], 1), ring(far.astype(BF16), 2)]
    else:
        got = [ring(pair[k], k) for k in range(1, ring_size())]
    return added([pair[0]] + [g.astype(F32) for g in got])


def whole(shape):
    return pl.BlockSpec(shape, lambda *_: (0,) * len(shape))


class Columns:
    def __init__(self, blocks, n, at=0):
        self.blocks, self.n, self.at = blocks, n, at

    def whole(self):
        rows, _, size, _ = self.blocks.shape
        at = self.at
        return pl.BlockSpec((rows, 1, size, self.n), lambda g, b, c, *_: (0, c[0], 0, at))

    def block(self, k, f):
        per, at = self.blocks.shape[2] // f, self.at
        return pl.BlockSpec((1, 1, f, self.n), lambda g, b, c, *_: (b[k] // per, c[0], b[k] % per, at))


def core_index():
    return lax.axis_index("c").astype(jnp.int32).reshape(1)


def matrix(ref):
    return ref[...].reshape(-1, ref.shape[-1])


def assembled(shards, blocks_ref, out_ref):
    f = shards[0].shape[1]
    for s, shard in enumerate(shards):
        out_ref[:, pl.ds(pl.multiple_of(blocks_ref[s] * f, f), f)] = shard[...].astype(BF16)


def norm_kernel(slots, width, gelu, blocks_ref, core_ref, *refs):
    shards = refs[:slots]
    means_ref, spread_ref, gain_ref, shift_ref, own_ref, w_ref, bias_ref, rows_ref = refs[slots : slots + 8]
    out_ref, centred_ref, inverse_ref, products_ref, *hidden_refs = refs[slots + 8 :]
    f = shards[0].shape[1]
    tokens = own_ref.shape[0]
    for g in range(tokens // LANES):
        at = pl.ds(g * LANES, LANES)
        offsets = lax.dot_general(
            means_ref[g].astype(BF16),
            spread_ref[...],
            (((0,), (0,)), ((), ())),
            preferred_element_type=F32,
        )
        values = [shards[s][at, :].astype(F32) + offsets[:, s * f : (s + 1) * f] for s in range(slots)]
        mean = jnp.sum(added(values), axis=1, keepdims=True) / width
        values = [v - mean for v in values]
        squares = added([v * v for v in values])
        inverse = lax.rsqrt(jnp.sum(squares, axis=1, keepdims=True) / width + norm_eps)
        for s in range(slots):
            normed = values[s] * inverse * gain_ref[s] + shift_ref[s]
            out_ref[at, pl.ds(pl.multiple_of(blocks_ref[s] * f, f), f)] = normed.astype(BF16)
        centred_ref[at, :] = (own_ref[at, :] - mean) * inverse
        inverse_ref[at, :] = jnp.broadcast_to(inverse, (LANES, LANES))
    hidden = jnp.dot(out_ref[...], matrix(w_ref), preferred_element_type=F32) + bias_ref[...]

    @pl.when(pl.program_id(0) == 0)
    def _():
        products_ref[...] = jnp.dot(rows_ref[...], matrix(w_ref), preferred_element_type=F32)

    if gelu:
        upper_ref, active_ref = hidden_refs
        upper_ref[...] = hidden
        active_ref[...] = gelu_tanh(hidden).astype(BF16)
    else:
        hidden_refs[0][...] = hidden.astype(BF16)


def norm_matmul(shards, own, gain, shift, w, bias, rows_to_multiply, gelu):
    slots = len(shards)
    tokens, f = own.shape
    width = slots * f
    n = w.n
    groups = tokens // LANES
    means = jnp.stack([s[tokens : tokens + groups, :LANES] for s in shards], axis=1).astype(F32)
    spread = jnp.repeat(jnp.eye(slots, dtype=BF16), f, axis=1)
    tile = min(tokens, 256)
    rows = lambda columns: pl.BlockSpec((tile, columns), lambda g, *_: (g, 0))
    outs = [(width, BF16), (f, F32), (LANES, F32)]
    hidden_outs = [(n, F32), (n, BF16)] if gelu else [(n, BF16)]
    many = rows_to_multiply.shape[0]
    return pl.pallas_call(
        functools.partial(norm_kernel, slots, width, gelu),
        grid_spec=pltpu.PrefetchScalarGridSpec(
            num_scalar_prefetch=2,
            grid=(tokens // tile,),
            in_specs=[rows(f)] * slots
            + [
                pl.BlockSpec((tile // LANES, slots, LANES), lambda g, *_: (g, 0, 0)),
                whole((slots, width)),
                whole((slots, 1, f)),
                whole((slots, 1, f)),
                rows(f),
                w.whole(),
                whole((1, n)),
                whole((many, width)),
            ],
            out_specs=[rows(columns) for columns, _ in outs]
            + [whole((many, n))]
            + [rows(columns) for columns, _ in hidden_outs],
        ),
        out_shape=[jax.ShapeDtypeStruct((tokens, columns), kind) for columns, kind in outs]
        + [jax.ShapeDtypeStruct((many, n), F32)]
        + [jax.ShapeDtypeStruct((tokens, columns), kind) for columns, kind in hidden_outs],
        compiler_params=pltpu.CompilerParams(vmem_limit_bytes=60 * MIB),
        cost_estimate=cost(
            flops=2 * tokens * width * n, bytes_accessed=8 * tokens * width, transcendentals=tokens
        ),
        name="norm_matmul",
    )(
        slot_blocks(),
        core_index(),
        *shards,
        means,
        spread,
        gain.reshape(slots, 1, f),
        shift.reshape(slots, 1, f),
        own,
        w.blocks,
        bias.reshape(1, n),
        rows_to_multiply,
    )


def hidden_back_kernel(slots, blocks_ref, core_ref, *refs):
    shards = refs[:slots]
    w_ref, upper_ref, rows_ref, base_ref = refs[slots : slots + 4]
    out_ref, grad_ref, sums_ref, bias_ref = refs[slots + 4 :]
    assembled(shards, blocks_ref, out_ref)
    tokens = upper_ref.shape[0]
    u = upper_ref[...]
    k = math.sqrt(2.0 / math.pi)
    t = jnp.tanh(k * (u + 0.044715 * (u * u * u)))
    slope = 0.5 * (1.0 + t) + 0.5 * u * (1.0 - t * t) * (k * (1.0 + 3 * 0.044715 * (u * u)))
    grad = (jnp.dot(out_ref[...], matrix(w_ref), preferred_element_type=F32) * slope).astype(BF16)
    grad_ref[...] = grad
    wide = grad.astype(F32)
    second = (wide * (u - base_ref[...])).astype(BF16)
    by_columns = (((1,), (1,)), ((), ()))
    for g in range(tokens // LANES):
        at = slice(g * LANES, (g + 1) * LANES)
        first = lax.dot_general(rows_ref[...], grad[at], by_columns, preferred_element_type=F32)
        ones = jnp.ones(rows_ref.shape, BF16)
        other = lax.dot_general(ones, second[at], by_columns, preferred_element_type=F32)
        sums_ref[g, 0:1, :] = first[0:1] + first[1:2]
        sums_ref[g, 1:2, :] = other[0:1]
        sums_ref[g, 2:, :] = jnp.zeros((6, LANES), F32)

    @pl.when(pl.program_id(0) == 0)
    def _():
        bias_ref[...] = jnp.zeros(bias_ref.shape, F32)

    bias_ref[...] += jnp.broadcast_to(jnp.sum(wide, axis=0, keepdims=True), bias_ref.shape)


def hidden_back(shards, w, upper, product, base):
    slots = len(shards)
    f = shards[0].shape[1]
    tokens, n = upper.shape
    width = slots * f
    tile = min(tokens, 256)
    high = lax.reduce_precision(product, 8, 7)
    pair = jnp.stack([high, product - high]).astype(BF16)
    pair = jnp.pad(pair, ((0, 14), (0, 0)))
    rows = lambda columns: pl.BlockSpec((tile, columns), lambda g, *_: (g, 0))
    out, grad, sums, bias = pl.pallas_call(
        functools.partial(hidden_back_kernel, slots),
        grid_spec=pltpu.PrefetchScalarGridSpec(
            num_scalar_prefetch=2,
            grid=(tokens // tile,),
            in_specs=[rows(f)] * slots + [w.whole(), rows(n), whole((16, n)), whole((1, n))],
            out_specs=[
                rows(width),
                rows(n),
                pl.BlockSpec((tile // LANES, 8, LANES), lambda g, *_: (g, 0, 0)),
                whole((8, n)),
            ],
        ),
        out_shape=[
            jax.ShapeDtypeStruct((tokens, width), BF16),
            jax.ShapeDtypeStruct((tokens, n), BF16),
            jax.ShapeDtypeStruct((tokens // LANES, 8, LANES), F32),
            jax.ShapeDtypeStruct((8, n), F32),
        ],
        compiler_params=pltpu.CompilerParams(vmem_limit_bytes=60 * MIB),
        cost_estimate=cost(
            flops=2 * tokens * width * n, bytes_accessed=8 * tokens * width, transcendentals=tokens * n
        ),
        name="hidden_back",
    )(slot_blocks(), core_index(), *shards, w.blocks, upper, pair, base.reshape(1, n))
    extra = jnp.concatenate([sums[:, 0], sums[:, 1]], axis=0).astype(BF16)
    extra = jnp.pad(extra, ((0, PAD - extra.shape[0]), (0, f - LANES)))
    return out, grad, extra, bias[0]


def gather_matmul_kernel(slots, blocks_ref, core_ref, *refs):
    w_ref, out_ref, product_ref = refs[slots:]
    assembled(refs[:slots], blocks_ref, out_ref)
    product_ref[...] = jnp.dot(out_ref[...], matrix(w_ref), preferred_element_type=F32).astype(BF16)


def gather_matmul(shards, w):
    slots = len(shards)
    tokens, f = shards[0].shape
    width = slots * f
    n = w.n
    tile = min(tokens, 256)
    rows = lambda columns: pl.BlockSpec((tile, columns), lambda g, *_: (g, 0))
    return pl.pallas_call(
        functools.partial(gather_matmul_kernel, slots),
        grid_spec=pltpu.PrefetchScalarGridSpec(
            num_scalar_prefetch=2,
            grid=(tokens // tile,),
            in_specs=[rows(f)] * slots + [w.whole()],
            out_specs=[rows(width), rows(n)],
        ),
        out_shape=[
            jax.ShapeDtypeStruct((tokens, width), BF16),
            jax.ShapeDtypeStruct((tokens, n), BF16),
        ],
        compiler_params=pltpu.CompilerParams(vmem_limit_bytes=60 * MIB),
        cost_estimate=cost(
            flops=2 * tokens * width * n, bytes_accessed=6 * tokens * width, transcendentals=0
        ),
        name="gather_matmul",
    )(slot_blocks(), core_index(), *shards, w.blocks)


def pack_kernel(turned, *refs):
    out_ref = refs[-1]
    at = 0
    for turn, ref in zip(turned, refs):
        value = ref[0].T if turn else ref[0]
        out_ref[:, at : at + value.shape[1]] = value.astype(BF16)
        at += value.shape[1]


def pack(blocks, turned, layer):
    tile = min(blocks[0].shape[2 if turned[0] else 1], 256)
    rows = blocks[0].shape[2 if turned[0] else 1]
    counts = [b.shape[1 if t else 2] for b, t in zip(blocks, turned)]
    return pl.pallas_call(
        functools.partial(pack_kernel, turned),
        grid=(rows // tile,),
        in_specs=[
            pl.BlockSpec((1, n, tile), lambda g: (layer, 0, g))
            if t
            else pl.BlockSpec((1, tile, n), lambda g: (layer, g, 0))
            for n, t in zip(counts, turned)
        ],
        out_specs=pl.BlockSpec((tile, sum(counts)), lambda g: (g, 0)),
        out_shape=jax.ShapeDtypeStruct((rows, sum(counts)), BF16),
        compiler_params=pltpu.CompilerParams(vmem_limit_bytes=24 * MIB),
        cost_estimate=cost(
            flops=0, bytes_accessed=6 * rows * sum(counts), transcendentals=0
        ),
        name="pack",
    )(*blocks)


def unpack_kernel(layers, turned, counts, same_ref, *refs):
    outs = refs[2 * layers :]
    for layer in range(layers):

        @pl.when(pl.program_id(0) == layer)
        def _():
            own, received = refs[2 * layer][...].astype(F32), refs[2 * layer + 1][...].astype(F32)
            value = jnp.where(same_ref[0] == 1, own, received)
            at = 0
            for turn, count, out in zip(turned, counts, outs):
                piece = value[:, at : at + count]
                out[0] = piece.T if turn else piece
                at += count


def unpack(pairs, turned, counts):
    layers = len(pairs)
    rows, columns = pairs[0][0].shape
    tile = min(rows, 256)
    same = (lax.axis_index("c") == lax.axis_index("x")).astype(jnp.int32).reshape(1)
    return pl.pallas_call(
        functools.partial(unpack_kernel, layers, turned, counts),
        grid_spec=pltpu.PrefetchScalarGridSpec(
            num_scalar_prefetch=1,
            grid=(layers, rows // tile),
            in_specs=[
                pl.BlockSpec((tile, columns), lambda n, g, _, layer=layer: (jnp.where(n == layer, g, 0), 0))
                for layer in range(layers)
                for _ in range(2)
            ],
            out_specs=[
                pl.BlockSpec((1, n, tile), lambda n, g, _: (n, 0, g))
                if t
                else pl.BlockSpec((1, tile, n), lambda n, g, _: (n, g, 0))
                for n, t in zip(counts, turned)
            ],
        ),
        out_shape=[
            jax.ShapeDtypeStruct((layers, n, rows) if t else (layers, rows, n), F32)
            for n, t in zip(counts, turned)
        ],
        compiler_params=pltpu.CompilerParams(vmem_limit_bytes=32 * MIB),
        cost_estimate=cost(
            flops=0, bytes_accessed=8 * layers * rows * columns, transcendentals=0
        ),
        name="unpack",
    )(same, *[v for pair in pairs for v in pair])


def slot_matmul_kernel(count, tile, blocks_ref, core_ref, x_ref, *refs):
    weights, extra_ref, outs = refs[:count], refs[count], refs[count + 1 :]
    tokens = x_ref.shape[0]
    for w_ref, out_ref in zip(weights, outs):
        for g in range(tokens // tile):
            at = pl.ds(g * tile, tile)
            out_ref[at, :] = lax.dot_general(
                x_ref[at, :], matrix(w_ref), (((1,), (1,)), ((), ())), preferred_element_type=F32
            ).astype(BF16)
        out_ref[tokens:, :] = extra_ref[...]


def slot_matmul(x, w, extra, other):
    tokens, depth = x.shape
    n = ring_size()
    f = extra.shape[1]
    blocks = slot_blocks()[1 if other else 0 :: 2]
    tile = min(tokens, 512)
    return pl.pallas_call(
        functools.partial(slot_matmul_kernel, n, tile),
        grid_spec=pltpu.PrefetchScalarGridSpec(
            num_scalar_prefetch=2,
            grid=(1,),
            in_specs=[whole((tokens, depth))]
            + [w.block(k, f) for k in range(n)]
            + [whole((PAD, f))],
            out_specs=[whole((tokens + PAD, f))] * n,
        ),
        out_shape=[jax.ShapeDtypeStruct((tokens + PAD, f), BF16)] * n,
        compiler_params=pltpu.CompilerParams(vmem_limit_bytes=32 * MIB),
        cost_estimate=cost(
            flops=2 * tokens * depth * n * f,
            bytes_accessed=2 * (tokens * depth + n * f * (depth + tokens)),
            transcendentals=0,
        ),
        name="slot_matmul",
    )(blocks, core_index(), x, *[w.blocks] * n, extra)


def column_sum(x, w, extra):
    other = slot_matmul(x, w, extra, True)
    mine = slot_matmul(x, w, extra, False)
    return pair_blocks(mine, other)


def block_scores(query, key, row0, column0, length, slope):
    rows, columns = query.shape[0], key.shape[0]
    scores = lax.dot_general(
        query, key, (((1,), (1,)), ((), ())), preferred_element_type=F32
    ) * (1.0 / math.sqrt(HEAD_DIM))
    row = lax.broadcasted_iota(jnp.int32, (rows, columns), 0) + row0
    column = lax.broadcasted_iota(jnp.int32, (rows, columns), 1) + column0
    scores = scores - slope * (row - column).astype(F32)
    return jnp.where((column <= row) & (column < length), scores, masked_score)


def attend_kernel(chunk, tile, length_ref, slope_ref, q_ref, *refs):
    keys, values = refs[: chunk + 1], refs[chunk + 1 : 2 * chunk + 2]
    context_ref, log_ref = refs[2 * chunk + 2 :]
    h, g = pl.program_id(0), pl.program_id(1)
    span = keys[0].shape[0]
    for step in range(span // tile):

        @pl.when(g == step)
        def _():
            attend_tile(
                chunk, tile, step, length_ref[0], slope_ref[h], q_ref, keys, values, context_ref, log_ref
            )


def reach(chunk, m, tile, step, span):
    return span if m < chunk else (step + 1) * tile


def attend_tile(chunk, tile, step, length, slope, q_ref, keys, values, context_ref, log_ref):
    span = keys[0].shape[0]
    query = q_ref[...]
    ends = [reach(chunk, m, tile, step, span) for m in range(chunk + 1)]
    scores = [
        block_scores(query, keys[m][: ends[m]], chunk * span + step * tile, m * span, length, slope)
        for m in range(chunk + 1)
    ]
    highest = functools.reduce(jnp.maximum, [jnp.max(s, axis=1, keepdims=True) for s in scores])
    raised = [jnp.exp(s - highest) for s in scores]
    total = sum(jnp.sum(r, axis=1, keepdims=True) for r in raised)
    context = sum(
        jnp.dot((r / total).astype(BF16), v[:end], preferred_element_type=F32)
        for r, v, end in zip(raised, values, ends)
    )
    context_ref[...] = context.astype(BF16)
    log_ref[...] = jnp.broadcast_to(highest + jnp.log(total), log_ref.shape)


def attend(chunk, joined, length, slopes):
    span, columns = joined[0].shape
    heads = columns // (3 * HEAD_DIM)
    tile = min(span, 256)
    own = joined[chunk]
    return pl.pallas_call(
        functools.partial(attend_kernel, chunk, tile),
        grid_spec=pltpu.PrefetchScalarGridSpec(
            num_scalar_prefetch=2,
            grid=(heads, span // tile),
            in_specs=[pl.BlockSpec((tile, HEAD_DIM), lambda h, g, *_: (g, 3 * h))]
            + [pl.BlockSpec((span, HEAD_DIM), lambda h, g, *_: (0, 3 * h + 1))] * (chunk + 1)
            + [pl.BlockSpec((span, HEAD_DIM), lambda h, g, *_: (0, 3 * h + 2))] * (chunk + 1),
            out_specs=[pl.BlockSpec((tile, HEAD_DIM), lambda h, g, *_: (g, h))] * 2,
        ),
        out_shape=[
            jax.ShapeDtypeStruct((span, heads * HEAD_DIM), BF16),
            jax.ShapeDtypeStruct((span, heads * HEAD_DIM), F32),
        ],
        compiler_params=pltpu.CompilerParams(vmem_limit_bytes=32 * MIB),
        cost_estimate=cost(
            flops=4 * span * span * (chunk + 1) * heads * HEAD_DIM,
            bytes_accessed=8 * span * columns * (chunk + 1),
            transcendentals=span * span * (chunk + 1) * heads,
        ),
        name="attend",
    )(length, slopes, own, *joined[: chunk + 1], *joined[: chunk + 1])


def attend_back_kernel(chunk, last, tile, length_ref, slope_ref, q_ref, *refs):
    n = chunk + 1
    keys, values, refs = refs[:n], refs[n : 2 * n], refs[2 * n :]
    given = []
    if not last:
        given, refs = refs[:n], refs[n:]
    grad_ref, log_ref, refs = refs[0], refs[1], refs[2:]
    out_ref, sums, refs = refs[0], refs[1:n], refs[n:]
    key_sums, value_sums = refs[:n], refs[n:]
    h, g = pl.program_id(0), pl.program_id(1)
    span = keys[0].shape[0]
    d = HEAD_DIM

    @pl.when(g == 0)
    def _():
        for m in range(n):
            if last:
                key_sums[m][...] = jnp.zeros((span, d), F32)
                value_sums[m][...] = jnp.zeros((span, d), F32)
            else:
                key_sums[m][...] = given[m][:, :d]
                value_sums[m][...] = given[m][:, d:]

    for step in range(span // tile):

        @pl.when(g == step)
        def _():
            query_grad = attend_back_tile(
                chunk,
                tile,
                step,
                length_ref[0],
                slope_ref[h],
                (q_ref, grad_ref, log_ref),
                (keys, values, key_sums, value_sums),
            )
            out_ref[step * tile : (step + 1) * tile, :d] = query_grad.astype(BF16)

    factor = 1.0 / math.sqrt(d)

    @pl.when(g == pl.num_programs(1) - 1)
    def _():
        out_ref[:, d : 2 * d] = (key_sums[chunk][...] * factor).astype(BF16)
        out_ref[:, 2 * d :] = value_sums[chunk][...].astype(BF16)
        for m in range(chunk):
            sums[m][:, :d] = key_sums[m][...]
            sums[m][:, d:] = value_sums[m][...]


def attend_back_tile(chunk, tile, step, length, slope, own, others):
    q_ref, grad_ref, log_ref = own
    keys, values, key_sums, value_sums = others
    span, d = keys[0].shape
    query, grad = q_ref[...], grad_ref[...]
    log_total = log_ref[:, :1]
    by_rows = (((0,), (0,)), ((), ()))
    ends = [reach(chunk, m, tile, step, span) for m in range(chunk + 1)]
    chances, chance_grads = [], []
    for m, end in enumerate(ends):
        scores = block_scores(
            query, keys[m][:end], chunk * span + step * tile, m * span, length, slope
        )
        chances.append(jnp.exp(scores - log_total))
        chance_grads.append(
            lax.dot_general(grad, values[m][:end], (((1,), (1,)), ((), ())), preferred_element_type=F32)
        )
    row_dot = added([jnp.sum(p * c, axis=1, keepdims=True) for p, c in zip(chances, chance_grads)])
    query_grad = jnp.zeros((tile, d), F32)
    for m, end in enumerate(ends):
        value_sums[m][:end] += lax.dot_general(
            chances[m].astype(BF16), grad, by_rows, preferred_element_type=F32
        )
        score_grad = (chances[m] * (chance_grads[m] - row_dot)).astype(BF16)
        query_grad += jnp.dot(score_grad, keys[m][:end], preferred_element_type=F32)
        key_sums[m][:end] += lax.dot_general(score_grad, query, by_rows, preferred_element_type=F32)
    return query_grad * (1.0 / math.sqrt(d))


def attend_back(chunk, joined, given, context_grad, log_total, length, slopes):
    span, columns = joined[0].shape
    heads = columns // (3 * HEAD_DIM)
    tile = min(span, 256)
    n = chunk + 1
    last = given is None
    wide = pl.BlockSpec((span, 2 * HEAD_DIM), lambda h, g, *_: (0, h))
    tall = pl.BlockSpec((tile, HEAD_DIM), lambda h, g, *_: (g, h))
    outs = pl.pallas_call(
        functools.partial(attend_back_kernel, chunk, last, tile),
        grid_spec=pltpu.PrefetchScalarGridSpec(
            num_scalar_prefetch=2,
            grid=(heads, span // tile),
            in_specs=[pl.BlockSpec((tile, HEAD_DIM), lambda h, g, *_: (g, 3 * h))]
            + [pl.BlockSpec((span, HEAD_DIM), lambda h, g, *_: (0, 3 * h + 1))] * n
            + [pl.BlockSpec((span, HEAD_DIM), lambda h, g, *_: (0, 3 * h + 2))] * n
            + [wide] * (0 if last else n)
            + [tall, tall],
            out_specs=[pl.BlockSpec((span, 3 * HEAD_DIM), lambda h, g, *_: (0, h))] + [wide] * chunk,
            scratch_shapes=[pltpu.VMEM((span, HEAD_DIM), F32)] * (2 * n),
        ),
        out_shape=[jax.ShapeDtypeStruct((span, columns), BF16)]
        + [jax.ShapeDtypeStruct((span, heads * 2 * HEAD_DIM), F32)] * chunk,
        compiler_params=pltpu.CompilerParams(vmem_limit_bytes=32 * MIB),
        cost_estimate=cost(
            flops=10 * span * span * n * heads * HEAD_DIM,
            bytes_accessed=12 * span * columns * n,
            transcendentals=span * span * n * heads,
        ),
        name="attend_back",
    )(
        length,
        slopes,
        joined[chunk],
        *joined[:n],
        *joined[:n],
        *([] if last else given),
        context_grad,
        log_total,
    )
    return outs[0], list(outs[1:])


def rows_of(column):
    return column.reshape(-1, LANES)


def packed(value, rows, width):
    extra = jnp.pad(rows.astype(value.dtype), ((0, PAD - rows.shape[0]), (0, width - rows.shape[1])))
    return jnp.concatenate([value, extra], axis=0)


def shard_of(value):
    mean = lax.reduce_precision(jnp.mean(value, axis=1, keepdims=True), 8, 7)
    return packed((value - mean).astype(BF16), rows_of(mean), value.shape[1])


def rows_for_products(gain, shift):
    rows = []
    for value in (gain, shift):
        high = lax.reduce_precision(value, 8, 7)
        rows += [high.astype(BF16), (value - high).astype(BF16)]
    return jnp.pad(jnp.stack(rows), ((0, PAD - len(rows)), (0, 0)))


def sums_rows(first, second, width):
    extra = jnp.concatenate([rows_of(first), rows_of(second)], axis=0).astype(BF16)
    return jnp.pad(extra, ((0, PAD - extra.shape[0]), (0, width - extra.shape[1])))


def norm_backward(summed, centred, inverse, gain, width):
    tokens = centred.shape[0]
    groups = tokens // LANES
    gradient = summed[:tokens]
    first_sum = summed[tokens : tokens + groups, :LANES].reshape(tokens, 1)
    second_sum = summed[tokens + groups : tokens + 2 * groups, :LANES].reshape(tokens, 1)
    passed = inverse[:, :1] * (gradient * gain - first_sum / width - centred * (second_sum / width))
    return (passed, jnp.sum(gradient * centred, axis=0), jnp.sum(gradient, axis=0))


def added(items):
    return functools.reduce(jnp.add, items)


def three_parts(value):
    terms = []
    for _ in range(3):
        high = lax.reduce_precision(value, 8, 7)
        terms.append(high.astype(BF16))
        value = value - high
    return terms


def gather_weight(block):
    return lax.all_gather(block, ("rh", "c", "x"), axis=0, tiled=True)


def by_blocks(gathered, rows):
    return gathered.reshape(-1, 2, rows, gathered.shape[1])


def scatter_weight(term):
    return lax.psum_scatter(term, ("rh", "x"), scatter_dimension=0, tiled=True)


def swapped(value):
    return value, lax.ppermute(value, ("c", "x"), [(1, 2), (2, 1)])


def on_device(
    activations,
    cotangent,
    lengths,
    first_gain,
    first_shift,
    joined_weight,
    query_bias,
    value_bias,
    output_weight,
    output_bias,
    second_gain,
    second_shift,
    up_weight,
    up_bias,
    down_weight,
    down_bias,
):
    tokens, f = activations.shape
    layers = first_gain.shape[0]
    width = 2 * ring_size() * f
    heads_local = f // HEAD_DIM
    span = tokens // CHUNKS
    chunks = range(CHUNKS)

    def cut(value):
        return [value[k * span : (k + 1) * span] for k in chunks]

    masked = cotangent * (jnp.arange(tokens) < lengths[0]).reshape(tokens, 1)
    lengths = swap_roles(lengths)
    head_index = block_index() * heads_local + jnp.arange(heads_local)
    slopes = jnp.exp2(-8.0 * (head_index + 1).astype(F32) / HEADS)

    smalls = (
        first_gain,
        first_shift,
        query_bias,
        value_bias,
        output_bias,
        second_gain,
        second_shift,
        down_bias,
    )
    table = jnp.concatenate(
        [s.reshape(layers, 1, f) for s in smalls] + [up_bias.reshape(layers, -1, f)], axis=1
    )
    table_rows = table.shape[1]
    count = layers * table_rows
    table = jnp.concatenate(three_parts(table.reshape(count, f)), axis=0)
    table = jnp.pad(table, ((0, -table.shape[0] % PAD), (0, 0)))
    shards = [shard_of(v) for v in cut(activations)]
    shards[0] = jnp.concatenate([shards[0], table], axis=0)
    shards = [swap_roles(s) for s in shards]
    residual = [swap_roles(after(v, *shards)) for v in cut(activations)]

    packs = []
    for layer in range(layers):
        blocks = (
            pack((joined_weight, output_weight), (False, True), layer),
            pack((up_weight,), (False,), layer),
            pack((down_weight,), (True,), layer),
        )
        if layer == 0:
            blocks, _ = lax.optimization_barrier((blocks, shards))
        packs.append([gather_weight(b) for b in blocks])
        if layer == 0:
            gradient = [swap_roles(after(v, packs[0][0])) for v in cut(masked)]
    rows = joined_weight.shape[1]
    weights = []

    low_shards = [swap_roles(after(v.astype(BF16), *shards)) for v in cut(masked)]
    slots = [gather_slots(s) for s in shards]
    first_slots = [gather_slots(after(v, *[s[3] for s in slots])) for v in low_shards]
    held = jnp.stack([s[span + PAD :][: 3 * count] for s in slots[0]]).astype(F32)
    table = (held[:, :count] + held[:, count : 2 * count] + held[:, 2 * count :]).reshape(
        len(slots[0]), layers, table_rows, f
    )
    own_up = table[0, :, len(smalls) :].reshape(layers, -1)
    natural = table[slot_blocks()]
    product_rows = [
        [
            rows_for_products(*(natural[:, layer, n].reshape(width) for n in pair))
            for pair in ((0, 1), (5, 6))
        ]
        for layer in range(layers)
    ]

    no_rows = jnp.zeros((PAD, f), BF16)
    saved = []
    turn = ()
    for layer in range(layers):
        last = layer + 1 == layers
        first_w = by_blocks(packs[layer][0], rows)
        joined_w, output_w = Columns(first_w, 3 * f), Columns(first_w, f, 3)
        products = []
        gains = [table[:, layer, n] for n in range(len(smalls))]
        own = table[0, layer]
        zero = jnp.zeros((heads_local, HEAD_DIM), F32)
        joined_bias = jnp.stack(
            (own[2].reshape(heads_local, HEAD_DIM), zero, own[3].reshape(heads_local, HEAD_DIM)), axis=1
        ).reshape(3 * f)
        joined, kept = [], []
        for k in chunks:
            slots[k], _ = lax.optimization_barrier((slots[k], turn))
            normed_one, centred_one, inverse_one, product_one, hidden = norm_matmul(
                slots[k], residual[k], gains[0], gains[1], joined_w, joined_bias, product_rows[layer][0], False
            )
            joined.append(hidden)
            if layer == 0:
                joined[k] = after(joined[k], *first_slots[k])
            context, log_total = attend(k, joined, lengths, slopes)
            pair = column_sum(context, output_w, no_rows)
            turn = pair
            middle = residual[k] + ring_sum(pair)[:span] + own[4]
            slots[k] = gather_slots(shard_of(middle))
            kept.append([normed_one, centred_one, inverse_one, context, log_total, middle])
        up_w = Columns(by_blocks(after(packs[layer][1], turn), rows), up_weight.shape[2])
        for k in chunks:
            middle = kept[k].pop()
            slots[k], _ = lax.optimization_barrier((slots[k], turn))
            normed_two, centred_two, inverse_two, product_two, upper, activated = norm_matmul(
                slots[k], middle, gains[5], gains[6], up_w, own_up[layer], product_rows[layer][1], True
            )
            if k == 0:
                down_w = Columns(by_blocks(after(packs[layer][2], upper), rows), down_weight.shape[1])
            turn = (activated,)
            if not last:
                pair = column_sum(activated, down_w, no_rows)
                turn = pair
                residual[k] = middle + ring_sum(pair)[:span] + own[7]
                slots[k] = gather_slots(shard_of(residual[k]))
            kept[k] += [normed_two, centred_two, inverse_two, upper, activated, middle]
        weights.append((joined_w, output_w, up_w, down_w))
        saved.append((joined, joined_bias, kept, product_one, product_two))

    weight_terms = [None] * layers
    small_terms = [None] * layers
    result, last_pairs, back_middle = ([None] * CHUNKS for _ in range(3))
    last_down_w = weights[-1][3]
    middle_grad = [None] * CHUNKS
    passed_one = [None] * CHUNKS

    def term(pieces):
        return added(
            [jnp.einsum("td,tn->dn", a, b, preferred_element_type=F32) for a, b in pieces]
        ).astype(BF16)

    for layer in reversed(range(layers)):
        joined, joined_bias, kept, product_one, product_two = saved[layer]
        joined_w, output_w, up_w, down_w = weights[layer]
        own = table[0, layer]
        up_gain, up_shift = product_two[0] + product_two[1], product_two[2] + product_two[3]
        joined_gain, joined_shift = product_one[0] + product_one[1], product_one[2] + product_one[3]
        given = None
        middle_slots, smalls_of, down_ends, up_ends, joined_ends, output_ends = ([None] * CHUNKS for _ in range(6))
        for k in reversed(chunks):
            normed_two, centred_two, inverse_two, upper, activated, middle = kept[k][5:]
            down_bias_term = jnp.sum(gradient[k], axis=0)
            slots = first_slots[k]
            slots, _ = lax.optimization_barrier((slots, turn))
            low_gradient, upper_grad, extra, up_bias_term = hidden_back(
                slots, down_w, upper, up_gain, own_up[layer] + up_shift
            )
            pair = column_sum(upper_grad, up_w, extra)
            turn = pair
            down_ends[k] = (low_gradient, after(activated, pair))
            if layer == 0:
                last_active = after(saved[-1][2][k][9], pair)
                last_pairs[k] = column_sum(last_active, last_down_w, no_rows)
            normed_two_grad = ring_sum(pair)
            if layer == 0:
                normed_two_grad = after(normed_two_grad, last_pairs[k])
            if k == 0:
                down_term = term(down_ends)
                normed_two_grad = after(normed_two_grad, down_term)
                if layer + 1 < layers:
                    normed_two_grad = after(normed_two_grad, joint_sum, up_pair[1])
                    joint_pair = swapped(joint_sum)
                    weight_terms[layer + 1] = [joint_pair, up_pair, down_pair]
                down_sum = scatter_weight(down_term)
            passed_two, gain_two_term, shift_two_term = norm_backward(
                normed_two_grad, centred_two, inverse_two, own[5], width
            )
            middle_grad[k] = gradient[k] + passed_two
            output_bias_term = jnp.sum(middle_grad[k], axis=0)
            smalls_of[k] = [output_bias_term, gain_two_term, shift_two_term, down_bias_term, up_bias_term]
            up_ends[k] = (normed_two, after(upper_grad, middle_grad[k]))
            middle_slots[k] = gather_slots(middle_grad[k].astype(BF16))
        for k in reversed(chunks):
            normed_one, centred_one, inverse_one, context, log_total = kept[k][:5]
            slots = middle_slots[k]
            slots, _ = lax.optimization_barrier((slots, turn))
            if k == 0:
                up_term = term(up_ends)
                slots, _ = lax.optimization_barrier((slots, (up_term, down_sum)))
                up_sum = scatter_weight(up_term)
                down_pair = swapped(down_sum)
            low_middle, context_grad = gather_matmul(slots, output_w)
            if layer == 0:
                back_middle[k] = swap_roles(after(middle_grad[k], low_middle))
                last_total = ring_sum(after(last_pairs[k], slots))
                result[k] = saved[-1][2][k][10] + last_total[:span] + table[0, layers - 1, 7]
            joined_grad, given = attend_back(
                k, joined, given, context_grad, log_total, lengths, slopes
            )
            wide_grad = joined_grad.astype(F32)
            first_sum = jnp.sum(wide_grad * joined_gain, axis=1)
            second_sum = jnp.sum(
                wide_grad * (joined[k].astype(F32) - (joined_bias + joined_shift)), axis=1
            )
            joined_ends[k] = (normed_one, joined_grad)
            output_ends[k] = (low_middle, context)
            if k == 0 and layer == 0:
                first_term = jnp.concatenate([term(joined_ends), term(output_ends)], axis=1)
                first_sum = after(first_sum, first_term, result[k], back_middle, weight_terms[-1][0][1])
                back_result = [swap_roles(r) for r in result]
            pair = column_sum(joined_grad, joined_w, sums_rows(first_sum, second_sum, f))
            turn = pair
            normed_one_grad = ring_sum(pair)
            if k == 0:
                up_pair = swapped(up_sum)
            if k == 0 and layer == 0:
                normed_one_grad = after(
                    normed_one_grad, down_pair[1], back_result
                )
            if k == 0 and layer > 0:
                joined_ends[0] = (normed_one, after(joined_grad, pair))
                output_ends[0] = (low_middle, after(context, pair))
                first_term = jnp.concatenate([term(joined_ends), term(output_ends)], axis=1)
                normed_one_grad = after(normed_one_grad, first_term, up_sum, down_pair[1])
            if k == 0:
                joint_sum = scatter_weight(first_term)
            joined_bias_term = jnp.sum(joined_grad.astype(F32), axis=0).reshape(heads_local, 3, HEAD_DIM)
            passed_one[k], gain_one_term, shift_one_term = norm_backward(
                normed_one_grad, centred_one, inverse_one, own[0], width
            )
            gradient[k] = middle_grad[k] + passed_one[k]
            if layer > 0:
                first_slots[k] = gather_slots(gradient[k].astype(BF16))
            smalls_of[k] = jnp.concatenate(
                [
                    t.reshape(-1, f)
                    for t in (
                        gain_one_term,
                        shift_one_term,
                        joined_bias_term[:, 0],
                        joined_bias_term[:, 2],
                        *smalls_of[k],
                    )
                ],
                axis=0,
            )
        small_terms[layer] = added(smalls_of)
    back_passed = [swap_roles(p.astype(BF16)) for p in passed_one]
    small = jnp.stack(small_terms)
    for axis in ("rh", "x"):
        size = lax.axis_size(axis)
        small = small + added(
            [lax.ppermute(small, axis, [(r, r ^ k) for r in range(size)]) for k in range(1, size)]
        )
    same = lax.axis_index("c") == lax.axis_index("x")
    small = jnp.where(same, small, partner(small))

    input_grad = jnp.concatenate(
        [m + after(p, small).astype(F32) for m, p in zip(back_middle, back_passed)],
        axis=0,
    )
    weight_terms[0] = [swapped(joint_sum), up_pair, down_pair]
    joined_out, output_out = unpack([t[0] for t in weight_terms], (False, True), (3 * f, f))
    (up_out,) = unpack([t[1] for t in weight_terms], (False,), (up_weight.shape[2],))
    (down_out,) = unpack([t[2] for t in weight_terms], (True,), (down_weight.shape[1],))

    return (
        jnp.concatenate(back_result, axis=0),
        input_grad,
        small[:, 0],
        small[:, 1],
        joined_out,
        small[:, 2],
        small[:, 3],
        output_out,
        small[:, 4],
        small[:, 5],
        small[:, 6],
        up_out,
        small[:, 8:].reshape(layers, -1),
        down_out,
        small[:, 7],
    )


def solution(mesh):
    rows, columns = mesh.devices.shape
    inner = Mesh(mesh.devices.reshape(rows // 2, 2, columns // 2, 2), ("rh", "c", "t", "x"))
    row, col = ("rh", "c"), ("t", "x")
    return jax.shard_map(
        on_device,
        mesh=inner,
        in_specs=(
            P(row, col),
            P(row, col),
            P(row),
            P(None, col),
            P(None, col),
            P(None, row, col),
            P(None, col),
            P(None, col),
            P(None, col, row),
            P(None, col),
            P(None, col),
            P(None, col),
            P(None, row, col),
            P(None, col),
            P(None, col, row),
            P(None, col),
        ),
        out_specs=(
            P(row, col),
            P(row, col),
            P(None, col),
            P(None, col),
            P(None, row, col),
            P(None, col),
            P(None, col),
            P(None, col, row),
            P(None, col),
            P(None, col),
            P(None, col),
            P(None, row, col),
            P(None, col),
            P(None, col, row),
            P(None, col),
        ),
        check_vma=False,
    )
```

```python
import functools
import math

import jax
import jax.numpy as jnp
from jax import lax
from jax.experimental import pallas as pl
from jax.experimental.pallas import tpu as pltpu
from jax.sharding import Mesh
from jax.sharding import PartitionSpec as P

HEADS = 16
HEAD_DIM = 128
PAD = 16
LANES = 128
CHUNKS = 1
MIB = 2**20
SCALE = 0.25


def cost(flops, bytes_accessed, transcendentals):
    return pl.CostEstimate(
        flops=int(flops * SCALE),
        bytes_accessed=int(bytes_accessed * SCALE),
        transcendentals=int(transcendentals * SCALE),
    )

norm_eps = 1e-05
masked_score = -1e30

F32 = jnp.float32
BF16 = jnp.bfloat16


def gelu_tanh(value):
    return jax.nn.gelu(value, approximate=True)


def after(value, *earlier):
    return lax.optimization_barrier((value, earlier))[0]


def ring_size():
    return lax.axis_size("t")


def ring(value, k):
    return lax.ppermute(value, "t", [(i, i ^ k) for i in range(ring_size())])


def partner(value):
    return lax.ppermute(value, "c", [(0, 1), (1, 0)])


def swap_roles(value):
    same = lax.axis_index("c") == lax.axis_index("x")
    return jnp.where(same, value, lax.ppermute(value, ("c", "x"), [(1, 2), (2, 1)]))


def block_index():
    return lax.axis_index("t") * 2 + lax.axis_index("c")


def slot_blocks():
    return (jnp.arange(2 * ring_size(), dtype=jnp.int32) ^ block_index()).astype(jnp.int32)


def gather_slots(value):
    if ring_size() == 4:
        far = ring(value, 2)
        mine = [value, ring(value, 1), far, ring(far, 1)]
    else:
        mine = [value] + [ring(value, k) for k in range(1, ring_size())]
    return [v for m in mine for v in (m, partner(m))]


def pair_blocks(mine, other):
    pair = [m.astype(F32) + partner(o).astype(F32) for m, o in zip(mine, other)]
    return [pair[0]] + [p.astype(BF16) for p in pair[1:]]


def ring_sum(pair):
    if ring_size() == 4:
        far = pair[2].astype(F32) + ring(pair[3], 1).astype(F32)
        got = [ring(pair[1], 1), ring(far.astype(BF16), 2)]
    else:
        got = [ring(pair[k], k) for k in range(1, ring_size())]
    return added([pair[0]] + [g.astype(F32) for g in got])


def whole(shape):
    return pl.BlockSpec(shape, lambda *_: (0,) * len(shape))


class Columns:
    def __init__(self, blocks, n, at=0):
        self.blocks, self.n, self.at = blocks, n, at

    def whole(self):
        rows, _, size, _ = self.blocks.shape
        at = self.at
        return pl.BlockSpec((rows, 1, size, self.n), lambda g, b, c, *_: (0, c[0], 0, at))

    def block(self, k, f):
        per, at = self.blocks.shape[2] // f, self.at
        return pl.BlockSpec((1, 1, f, self.n), lambda g, b, c, *_: (b[k] // per, c[0], b[k] % per, at))


def core_index():
    return lax.axis_index("c").astype(jnp.int32).reshape(1)


def matrix(ref):
    return ref[...].reshape(-1, ref.shape[-1])


def assembled(shards, blocks_ref, out_ref):
    f = shards[0].shape[1]
    for s, shard in enumerate(shards):
        out_ref[:, pl.ds(pl.multiple_of(blocks_ref[s] * f, f), f)] = shard[...].astype(BF16)


def norm_kernel(slots, width, gelu, blocks_ref, core_ref, *refs):
    shards = refs[:slots]
    means_ref, spread_ref, gain_ref, shift_ref, own_ref, w_ref, bias_ref, rows_ref = refs[slots : slots + 8]
    out_ref, centred_ref, inverse_ref, products_ref, *hidden_refs = refs[slots + 8 :]
    f = shards[0].shape[1]
    tokens = own_ref.shape[0]
    for g in range(tokens // LANES):
        at = pl.ds(g * LANES, LANES)
        offsets = lax.dot_general(
            means_ref[g].astype(BF16),
            spread_ref[...],
            (((0,), (0,)), ((), ())),
            preferred_element_type=F32,
        )
        values = [shards[s][at, :].astype(F32) + offsets[:, s * f : (s + 1) * f] for s in range(slots)]
        mean = jnp.sum(added(values), axis=1, keepdims=True) / width
        values = [v - mean for v in values]
        squares = added([v * v for v in values])
        inverse = lax.rsqrt(jnp.sum(squares, axis=1, keepdims=True) / width + norm_eps)
        for s in range(slots):
            normed = values[s] * inverse * gain_ref[s] + shift_ref[s]
            out_ref[at, pl.ds(pl.multiple_of(blocks_ref[s] * f, f), f)] = normed.astype(BF16)
        centred_ref[at, :] = (own_ref[at, :] - mean) * inverse
        inverse_ref[at, :] = jnp.broadcast_to(inverse, (LANES, LANES))
    hidden = jnp.dot(out_ref[...], matrix(w_ref), preferred_element_type=F32) + bias_ref[...]

    @pl.when(pl.program_id(0) == 0)
    def _():
        products_ref[...] = jnp.dot(rows_ref[...], matrix(w_ref), preferred_element_type=F32)

    if gelu:
        upper_ref, active_ref = hidden_refs
        upper_ref[...] = hidden
        active_ref[...] = gelu_tanh(hidden).astype(BF16)
    else:
        hidden_refs[0][...] = hidden.astype(BF16)


def norm_matmul(shards, own, gain, shift, w, bias, rows_to_multiply, gelu):
    slots = len(shards)
    tokens, f = own.shape
    width = slots * f
    n = w.n
    groups = tokens // LANES
    means = jnp.stack([s[tokens : tokens + groups, :LANES] for s in shards], axis=1).astype(F32)
    spread = jnp.repeat(jnp.eye(slots, dtype=BF16), f, axis=1)
    tile = min(tokens, 256)
    rows = lambda columns: pl.BlockSpec((tile, columns), lambda g, *_: (g, 0))
    outs = [(width, BF16), (f, F32), (LANES, F32)]
    hidden_outs = [(n, F32), (n, BF16)] if gelu else [(n, BF16)]
    many = rows_to_multiply.shape[0]
    return pl.pallas_call(
        functools.partial(norm_kernel, slots, width, gelu),
        grid_spec=pltpu.PrefetchScalarGridSpec(
            num_scalar_prefetch=2,
            grid=(tokens // tile,),
            in_specs=[rows(f)] * slots
            + [
                pl.BlockSpec((tile // LANES, slots, LANES), lambda g, *_: (g, 0, 0)),
                whole((slots, width)),
                whole((slots, 1, f)),
                whole((slots, 1, f)),
                rows(f),
                w.whole(),
                whole((1, n)),
                whole((many, width)),
            ],
            out_specs=[rows(columns) for columns, _ in outs]
            + [whole((many, n))]
            + [rows(columns) for columns, _ in hidden_outs],
        ),
        out_shape=[jax.ShapeDtypeStruct((tokens, columns), kind) for columns, kind in outs]
        + [jax.ShapeDtypeStruct((many, n), F32)]
        + [jax.ShapeDtypeStruct((tokens, columns), kind) for columns, kind in hidden_outs],
        compiler_params=pltpu.CompilerParams(vmem_limit_bytes=60 * MIB),
        cost_estimate=cost(
            flops=2 * tokens * width * n, bytes_accessed=8 * tokens * width, transcendentals=tokens
        ),
        name="norm_matmul",
    )(
        slot_blocks(),
        core_index(),
        *shards,
        means,
        spread,
        gain.reshape(slots, 1, f),
        shift.reshape(slots, 1, f),
        own,
        w.blocks,
        bias.reshape(1, n),
        rows_to_multiply,
    )


def hidden_back_kernel(slots, blocks_ref, core_ref, *refs):
    shards = refs[:slots]
    w_ref, upper_ref, rows_ref, base_ref = refs[slots : slots + 4]
    out_ref, grad_ref, sums_ref, bias_ref = refs[slots + 4 :]
    assembled(shards, blocks_ref, out_ref)
    tokens = upper_ref.shape[0]
    u = upper_ref[...]
    k = math.sqrt(2.0 / math.pi)
    t = jnp.tanh(k * (u + 0.044715 * (u * u * u)))
    slope = 0.5 * (1.0 + t) + 0.5 * u * (1.0 - t * t) * (k * (1.0 + 3 * 0.044715 * (u * u)))
    grad = (jnp.dot(out_ref[...], matrix(w_ref), preferred_element_type=F32) * slope).astype(BF16)
    grad_ref[...] = grad
    wide = grad.astype(F32)
    second = (wide * (u - base_ref[...])).astype(BF16)
    by_columns = (((1,), (1,)), ((), ()))
    for g in range(tokens // LANES):
        at = slice(g * LANES, (g + 1) * LANES)
        first = lax.dot_general(rows_ref[...], grad[at], by_columns, preferred_element_type=F32)
        ones = jnp.ones(rows_ref.shape, BF16)
        other = lax.dot_general(ones, second[at], by_columns, preferred_element_type=F32)
        sums_ref[g, 0:1, :] = first[0:1] + first[1:2]
        sums_ref[g, 1:2, :] = other[0:1]
        sums_ref[g, 2:, :] = jnp.zeros((6, LANES), F32)

    @pl.when(pl.program_id(0) == 0)
    def _():
        bias_ref[...] = jnp.zeros(bias_ref.shape, F32)

    bias_ref[...] += jnp.broadcast_to(jnp.sum(wide, axis=0, keepdims=True), bias_ref.shape)


def hidden_back(shards, w, upper, product, base):
    slots = len(shards)
    f = shards[0].shape[1]
    tokens, n = upper.shape
    width = slots * f
    tile = min(tokens, 256)
    high = lax.reduce_precision(product, 8, 7)
    pair = jnp.stack([high, product - high]).astype(BF16)
    pair = jnp.pad(pair, ((0, 14), (0, 0)))
    rows = lambda columns: pl.BlockSpec((tile, columns), lambda g, *_: (g, 0))
    out, grad, sums, bias = pl.pallas_call(
        functools.partial(hidden_back_kernel, slots),
        grid_spec=pltpu.PrefetchScalarGridSpec(
            num_scalar_prefetch=2,
            grid=(tokens // tile,),
            in_specs=[rows(f)] * slots + [w.whole(), rows(n), whole((16, n)), whole((1, n))],
            out_specs=[
                rows(width),
                rows(n),
                pl.BlockSpec((tile // LANES, 8, LANES), lambda g, *_: (g, 0, 0)),
                whole((8, n)),
            ],
        ),
        out_shape=[
            jax.ShapeDtypeStruct((tokens, width), BF16),
            jax.ShapeDtypeStruct((tokens, n), BF16),
            jax.ShapeDtypeStruct((tokens // LANES, 8, LANES), F32),
            jax.ShapeDtypeStruct((8, n), F32),
        ],
        compiler_params=pltpu.CompilerParams(vmem_limit_bytes=60 * MIB),
        cost_estimate=cost(
            flops=2 * tokens * width * n, bytes_accessed=8 * tokens * width, transcendentals=tokens * n
        ),
        name="hidden_back",
    )(slot_blocks(), core_index(), *shards, w.blocks, upper, pair, base.reshape(1, n))
    extra = jnp.concatenate([sums[:, 0], sums[:, 1]], axis=0).astype(BF16)
    extra = jnp.pad(extra, ((0, PAD - extra.shape[0]), (0, f - LANES)))
    return out, grad, extra, bias[0]


def gather_matmul_kernel(slots, blocks_ref, core_ref, *refs):
    w_ref, out_ref, product_ref = refs[slots:]
    assembled(refs[:slots], blocks_ref, out_ref)
    product_ref[...] = jnp.dot(out_ref[...], matrix(w_ref), preferred_element_type=F32).astype(BF16)


def gather_matmul(shards, w):
    slots = len(shards)
    tokens, f = shards[0].shape
    width = slots * f
    n = w.n
    tile = min(tokens, 256)
    rows = lambda columns: pl.BlockSpec((tile, columns), lambda g, *_: (g, 0))
    return pl.pallas_call(
        functools.partial(gather_matmul_kernel, slots),
        grid_spec=pltpu.PrefetchScalarGridSpec(
            num_scalar_prefetch=2,
            grid=(tokens // tile,),
            in_specs=[rows(f)] * slots + [w.whole()],
            out_specs=[rows(width), rows(n)],
        ),
        out_shape=[
            jax.ShapeDtypeStruct((tokens, width), BF16),
            jax.ShapeDtypeStruct((tokens, n), BF16),
        ],
        compiler_params=pltpu.CompilerParams(vmem_limit_bytes=60 * MIB),
        cost_estimate=cost(
            flops=2 * tokens * width * n, bytes_accessed=6 * tokens * width, transcendentals=0
        ),
        name="gather_matmul",
    )(slot_blocks(), core_index(), *shards, w.blocks)


def pack_kernel(turned, *refs):
    out_ref = refs[-1]
    at = 0
    for turn, ref in zip(turned, refs):
        value = ref[0].T if turn else ref[0]
        out_ref[:, at : at + value.shape[1]] = value.astype(BF16)
        at += value.shape[1]


def pack(blocks, turned, layer):
    tile = min(blocks[0].shape[2 if turned[0] else 1], 256)
    rows = blocks[0].shape[2 if turned[0] else 1]
    counts = [b.shape[1 if t else 2] for b, t in zip(blocks, turned)]
    return pl.pallas_call(
        functools.partial(pack_kernel, turned),
        grid=(rows // tile,),
        in_specs=[
            pl.BlockSpec((1, n, tile), lambda g: (layer, 0, g))
            if t
            else pl.BlockSpec((1, tile, n), lambda g: (layer, g, 0))
            for n, t in zip(counts, turned)
        ],
        out_specs=pl.BlockSpec((tile, sum(counts)), lambda g: (g, 0)),
        out_shape=jax.ShapeDtypeStruct((rows, sum(counts)), BF16),
        compiler_params=pltpu.CompilerParams(vmem_limit_bytes=24 * MIB),
        cost_estimate=cost(
            flops=0, bytes_accessed=6 * rows * sum(counts), transcendentals=0
        ),
        name="pack",
    )(*blocks)


def unpack_kernel(layers, turned, counts, same_ref, *refs):
    outs = refs[2 * layers :]
    for layer in range(layers):

        @pl.when(pl.program_id(0) == layer)
        def _():
            own, received = refs[2 * layer][...].astype(F32), refs[2 * layer + 1][...].astype(F32)
            value = jnp.where(same_ref[0] == 1, own, received)
            at = 0
            for turn, count, out in zip(turned, counts, outs):
                piece = value[:, at : at + count]
                out[0] = piece.T if turn else piece
                at += count


def unpack(pairs, turned, counts):
    layers = len(pairs)
    rows, columns = pairs[0][0].shape
    tile = min(rows, 256)
    same = (lax.axis_index("c") == lax.axis_index("x")).astype(jnp.int32).reshape(1)
    return pl.pallas_call(
        functools.partial(unpack_kernel, layers, turned, counts),
        grid_spec=pltpu.PrefetchScalarGridSpec(
            num_scalar_prefetch=1,
            grid=(layers, rows // tile),
            in_specs=[
                pl.BlockSpec((tile, columns), lambda n, g, _, layer=layer: (jnp.where(n == layer, g, 0), 0))
                for layer in range(layers)
                for _ in range(2)
            ],
            out_specs=[
                pl.BlockSpec((1, n, tile), lambda n, g, _: (n, 0, g))
                if t
                else pl.BlockSpec((1, tile, n), lambda n, g, _: (n, g, 0))
                for n, t in zip(counts, turned)
            ],
        ),
        out_shape=[
            jax.ShapeDtypeStruct((layers, n, rows) if t else (layers, rows, n), F32)
            for n, t in zip(counts, turned)
        ],
        compiler_params=pltpu.CompilerParams(vmem_limit_bytes=32 * MIB),
        cost_estimate=cost(
            flops=0, bytes_accessed=8 * layers * rows * columns, transcendentals=0
        ),
        name="unpack",
    )(same, *[v for pair in pairs for v in pair])


def slot_matmul_kernel(count, tile, blocks_ref, core_ref, x_ref, *refs):
    weights, extra_ref, outs = refs[:count], refs[count], refs[count + 1 :]
    tokens = x_ref.shape[0]
    for w_ref, out_ref in zip(weights, outs):
        for g in range(tokens // tile):
            at = pl.ds(g * tile, tile)
            out_ref[at, :] = lax.dot_general(
                x_ref[at, :], matrix(w_ref), (((1,), (1,)), ((), ())), preferred_element_type=F32
            ).astype(BF16)
        out_ref[tokens:, :] = extra_ref[...]


def slot_matmul(x, w, extra):
    tokens, depth = x.shape
    n = 2 * ring_size()
    f = extra.shape[1]
    blocks = slot_blocks()
    blocks = jnp.concatenate([blocks[1::2], blocks[::2]])
    tile = min(tokens, 512)
    outs = pl.pallas_call(
        functools.partial(slot_matmul_kernel, n, tile),
        grid_spec=pltpu.PrefetchScalarGridSpec(
            num_scalar_prefetch=2,
            grid=(1,),
            in_specs=[whole((tokens, depth))]
            + [w.block(k, f) for k in range(n)]
            + [whole((PAD, f))],
            out_specs=[whole((tokens + PAD, f))] * n,
        ),
        out_shape=[jax.ShapeDtypeStruct((tokens + PAD, f), BF16)] * n,
        compiler_params=pltpu.CompilerParams(vmem_limit_bytes=32 * MIB),
        cost_estimate=cost(
            flops=2 * tokens * depth * n * f,
            bytes_accessed=2 * (tokens * depth + n * f * (depth + tokens)),
            transcendentals=0,
        ),
        name="slot_matmul",
    )(blocks, core_index(), x, *[w.blocks] * n, extra)
    return outs[n // 2 :], outs[: n // 2]


def column_sum(x, w, extra):
    return pair_blocks(*slot_matmul(x, w, extra))


def block_scores(query, key, row0, column0, length, slope):
    rows, columns = query.shape[0], key.shape[0]
    scores = lax.dot_general(
        query, key, (((1,), (1,)), ((), ())), preferred_element_type=F32
    ) * (1.0 / math.sqrt(HEAD_DIM))
    row = lax.broadcasted_iota(jnp.int32, (rows, columns), 0) + row0
    column = lax.broadcasted_iota(jnp.int32, (rows, columns), 1) + column0
    scores = scores - slope * (row - column).astype(F32)
    return jnp.where((column <= row) & (column < length), scores, masked_score)


def attend_kernel(chunk, tile, length_ref, slope_ref, q_ref, *refs):
    keys, values = refs[: chunk + 1], refs[chunk + 1 : 2 * chunk + 2]
    context_ref, log_ref = refs[2 * chunk + 2 :]
    h, g = pl.program_id(0), pl.program_id(1)
    span = keys[0].shape[0]
    for step in range(span // tile):

        @pl.when(g == step)
        def _():
            attend_tile(
                chunk, tile, step, length_ref[0], slope_ref[h], q_ref, keys, values, context_ref, log_ref
            )


def reach(chunk, m, tile, step, span):
    return span if m < chunk else (step + 1) * tile


def attend_tile(chunk, tile, step, length, slope, q_ref, keys, values, context_ref, log_ref):
    span = keys[0].shape[0]
    query = q_ref[...]
    ends = [reach(chunk, m, tile, step, span) for m in range(chunk + 1)]
    scores = [
        block_scores(query, keys[m][: ends[m]], chunk * span + step * tile, m * span, length, slope)
        for m in range(chunk + 1)
    ]
    highest = functools.reduce(jnp.maximum, [jnp.max(s, axis=1, keepdims=True) for s in scores])
    raised = [jnp.exp(s - highest) for s in scores]
    total = sum(jnp.sum(r, axis=1, keepdims=True) for r in raised)
    context = sum(
        jnp.dot((r / total).astype(BF16), v[:end], preferred_element_type=F32)
        for r, v, end in zip(raised, values, ends)
    )
    context_ref[...] = context.astype(BF16)
    log_ref[...] = jnp.broadcast_to(highest + jnp.log(total), log_ref.shape)


def attend(chunk, joined, length, slopes):
    span, columns = joined[0].shape
    heads = columns // (3 * HEAD_DIM)
    tile = min(span, 256)
    own = joined[chunk]
    return pl.pallas_call(
        functools.partial(attend_kernel, chunk, tile),
        grid_spec=pltpu.PrefetchScalarGridSpec(
            num_scalar_prefetch=2,
            grid=(heads, span // tile),
            in_specs=[pl.BlockSpec((tile, HEAD_DIM), lambda h, g, *_: (g, 3 * h))]
            + [pl.BlockSpec((span, HEAD_DIM), lambda h, g, *_: (0, 3 * h + 1))] * (chunk + 1)
            + [pl.BlockSpec((span, HEAD_DIM), lambda h, g, *_: (0, 3 * h + 2))] * (chunk + 1),
            out_specs=[pl.BlockSpec((tile, HEAD_DIM), lambda h, g, *_: (g, h))] * 2,
        ),
        out_shape=[
            jax.ShapeDtypeStruct((span, heads * HEAD_DIM), BF16),
            jax.ShapeDtypeStruct((span, heads * HEAD_DIM), F32),
        ],
        compiler_params=pltpu.CompilerParams(vmem_limit_bytes=32 * MIB),
        cost_estimate=cost(
            flops=4 * span * span * (chunk + 1) * heads * HEAD_DIM,
            bytes_accessed=8 * span * columns * (chunk + 1),
            transcendentals=span * span * (chunk + 1) * heads,
        ),
        name="attend",
    )(length, slopes, own, *joined[: chunk + 1], *joined[: chunk + 1])


def attend_back_kernel(chunk, last, tile, length_ref, slope_ref, q_ref, *refs):
    n = chunk + 1
    keys, values, refs = refs[:n], refs[n : 2 * n], refs[2 * n :]
    given = []
    if not last:
        given, refs = refs[:n], refs[n:]
    grad_ref, log_ref, refs = refs[0], refs[1], refs[2:]
    out_ref, sums, refs = refs[0], refs[1:n], refs[n:]
    key_sums, value_sums = refs[:n], refs[n:]
    h, g = pl.program_id(0), pl.program_id(1)
    span = keys[0].shape[0]
    d = HEAD_DIM

    @pl.when(g == 0)
    def _():
        for m in range(n):
            if last:
                key_sums[m][...] = jnp.zeros((span, d), F32)
                value_sums[m][...] = jnp.zeros((span, d), F32)
            else:
                key_sums[m][...] = given[m][:, :d]
                value_sums[m][...] = given[m][:, d:]

    for step in range(span // tile):

        @pl.when(g == step)
        def _():
            query_grad = attend_back_tile(
                chunk,
                tile,
                step,
                length_ref[0],
                slope_ref[h],
                (q_ref, grad_ref, log_ref),
                (keys, values, key_sums, value_sums),
            )
            out_ref[step * tile : (step + 1) * tile, :d] = query_grad.astype(BF16)

    factor = 1.0 / math.sqrt(d)

    @pl.when(g == pl.num_programs(1) - 1)
    def _():
        out_ref[:, d : 2 * d] = (key_sums[chunk][...] * factor).astype(BF16)
        out_ref[:, 2 * d :] = value_sums[chunk][...].astype(BF16)
        for m in range(chunk):
            sums[m][:, :d] = key_sums[m][...]
            sums[m][:, d:] = value_sums[m][...]


def attend_back_tile(chunk, tile, step, length, slope, own, others):
    q_ref, grad_ref, log_ref = own
    keys, values, key_sums, value_sums = others
    span, d = keys[0].shape
    query, grad = q_ref[...], grad_ref[...]
    log_total = log_ref[:, :1]
    by_rows = (((0,), (0,)), ((), ()))
    ends = [reach(chunk, m, tile, step, span) for m in range(chunk + 1)]
    chances, chance_grads = [], []
    for m, end in enumerate(ends):
        scores = block_scores(
            query, keys[m][:end], chunk * span + step * tile, m * span, length, slope
        )
        chances.append(jnp.exp(scores - log_total))
        chance_grads.append(
            lax.dot_general(grad, values[m][:end], (((1,), (1,)), ((), ())), preferred_element_type=F32)
        )
    row_dot = added([jnp.sum(p * c, axis=1, keepdims=True) for p, c in zip(chances, chance_grads)])
    query_grad = jnp.zeros((tile, d), F32)
    for m, end in enumerate(ends):
        value_sums[m][:end] += lax.dot_general(
            chances[m].astype(BF16), grad, by_rows, preferred_element_type=F32
        )
        score_grad = (chances[m] * (chance_grads[m] - row_dot)).astype(BF16)
        query_grad += jnp.dot(score_grad, keys[m][:end], preferred_element_type=F32)
        key_sums[m][:end] += lax.dot_general(score_grad, query, by_rows, preferred_element_type=F32)
    return query_grad * (1.0 / math.sqrt(d))


def attend_back(chunk, joined, given, context_grad, log_total, length, slopes):
    span, columns = joined[0].shape
    heads = columns // (3 * HEAD_DIM)
    tile = min(span, 256)
    n = chunk + 1
    last = given is None
    wide = pl.BlockSpec((span, 2 * HEAD_DIM), lambda h, g, *_: (0, h))
    tall = pl.BlockSpec((tile, HEAD_DIM), lambda h, g, *_: (g, h))
    outs = pl.pallas_call(
        functools.partial(attend_back_kernel, chunk, last, tile),
        grid_spec=pltpu.PrefetchScalarGridSpec(
            num_scalar_prefetch=2,
            grid=(heads, span // tile),
            in_specs=[pl.BlockSpec((tile, HEAD_DIM), lambda h, g, *_: (g, 3 * h))]
            + [pl.BlockSpec((span, HEAD_DIM), lambda h, g, *_: (0, 3 * h + 1))] * n
            + [pl.BlockSpec((span, HEAD_DIM), lambda h, g, *_: (0, 3 * h + 2))] * n
            + [wide] * (0 if last else n)
            + [tall, tall],
            out_specs=[pl.BlockSpec((span, 3 * HEAD_DIM), lambda h, g, *_: (0, h))] + [wide] * chunk,
            scratch_shapes=[pltpu.VMEM((span, HEAD_DIM), F32)] * (2 * n),
        ),
        out_shape=[jax.ShapeDtypeStruct((span, columns), BF16)]
        + [jax.ShapeDtypeStruct((span, heads * 2 * HEAD_DIM), F32)] * chunk,
        compiler_params=pltpu.CompilerParams(vmem_limit_bytes=32 * MIB),
        cost_estimate=cost(
            flops=10 * span * span * n * heads * HEAD_DIM,
            bytes_accessed=12 * span * columns * n,
            transcendentals=span * span * n * heads,
        ),
        name="attend_back",
    )(
        length,
        slopes,
        joined[chunk],
        *joined[:n],
        *joined[:n],
        *([] if last else given),
        context_grad,
        log_total,
    )
    return outs[0], list(outs[1:])


def rows_of(column):
    return column.reshape(-1, LANES)


def packed(value, rows, width):
    extra = jnp.pad(rows.astype(value.dtype), ((0, PAD - rows.shape[0]), (0, width - rows.shape[1])))
    return jnp.concatenate([value, extra], axis=0)


def shard_of(value):
    mean = lax.reduce_precision(jnp.mean(value, axis=1, keepdims=True), 8, 7)
    return packed((value - mean).astype(BF16), rows_of(mean), value.shape[1])


def rows_for_products(gain, shift):
    rows = []
    for value in (gain, shift):
        high = lax.reduce_precision(value, 8, 7)
        rows += [high.astype(BF16), (value - high).astype(BF16)]
    return jnp.pad(jnp.stack(rows), ((0, PAD - len(rows)), (0, 0)))


def sums_rows(first, second, width):
    extra = jnp.concatenate([rows_of(first), rows_of(second)], axis=0).astype(BF16)
    return jnp.pad(extra, ((0, PAD - extra.shape[0]), (0, width - extra.shape[1])))


def norm_backward(summed, centred, inverse, gain, width):
    tokens = centred.shape[0]
    groups = tokens // LANES
    gradient = summed[:tokens]
    first_sum = summed[tokens : tokens + groups, :LANES].reshape(tokens, 1)
    second_sum = summed[tokens + groups : tokens + 2 * groups, :LANES].reshape(tokens, 1)
    passed = inverse[:, :1] * (gradient * gain - first_sum / width - centred * (second_sum / width))
    return (passed, jnp.sum(gradient * centred, axis=0), jnp.sum(gradient, axis=0))


def added(items):
    return functools.reduce(jnp.add, items)


def three_parts(value):
    terms = []
    for _ in range(3):
        high = lax.reduce_precision(value, 8, 7)
        terms.append(high.astype(BF16))
        value = value - high
    return terms


def gather_weight(block):
    return lax.all_gather(block, ("rh", "c", "x"), axis=0, tiled=True)


def by_blocks(gathered, rows):
    return gathered.reshape(-1, 2, rows, gathered.shape[1])


def scatter_weight(term):
    return lax.psum_scatter(term, ("rh", "x"), scatter_dimension=0, tiled=True)


def swapped(value):
    return value, lax.ppermute(value, ("c", "x"), [(1, 2), (2, 1)])


def on_device(
    activations,
    cotangent,
    lengths,
    first_gain,
    first_shift,
    joined_weight,
    query_bias,
    value_bias,
    output_weight,
    output_bias,
    second_gain,
    second_shift,
    up_weight,
    up_bias,
    down_weight,
    down_bias,
):
    tokens, f = activations.shape
    layers = first_gain.shape[0]
    width = 2 * ring_size() * f
    heads_local = f // HEAD_DIM
    span = tokens // CHUNKS
    chunks = range(CHUNKS)

    def cut(value):
        return [value[k * span : (k + 1) * span] for k in chunks]

    masked = cotangent * (jnp.arange(tokens) < lengths[0]).reshape(tokens, 1)
    lengths = swap_roles(lengths)
    head_index = block_index() * heads_local + jnp.arange(heads_local)
    slopes = jnp.exp2(-8.0 * (head_index + 1).astype(F32) / HEADS)

    smalls = (
        first_gain,
        first_shift,
        query_bias,
        value_bias,
        output_bias,
        second_gain,
        second_shift,
        down_bias,
    )
    table = jnp.concatenate(
        [s.reshape(layers, 1, f) for s in smalls] + [up_bias.reshape(layers, -1, f)], axis=1
    )
    table_rows = table.shape[1]
    count = layers * table_rows
    table = jnp.concatenate(three_parts(table.reshape(count, f)), axis=0)
    table = jnp.pad(table, ((0, -table.shape[0] % PAD), (0, 0)))
    shards = [shard_of(v) for v in cut(activations)]
    shards[0] = jnp.concatenate([shards[0], table], axis=0)
    shards = [swap_roles(s) for s in shards]
    residual = [swap_roles(after(v, *shards)) for v in cut(activations)]

    packs = []
    for layer in range(layers):
        blocks = (
            pack((joined_weight, output_weight), (False, True), layer),
            pack((up_weight,), (False,), layer),
            pack((down_weight,), (True,), layer),
        )
        if layer == 0:
            blocks, _ = lax.optimization_barrier((blocks, shards))
        packs.append([gather_weight(b) for b in blocks])
        if layer == 0:
            gradient = [swap_roles(after(v, packs[0][0])) for v in cut(masked)]
    rows = joined_weight.shape[1]
    weights = []

    low_shards = [swap_roles(after(v.astype(BF16), *shards)) for v in cut(masked)]
    slots = [gather_slots(s) for s in shards]
    first_slots = [gather_slots(after(v, *[s[3] for s in slots])) for v in low_shards]
    held = jnp.stack([s[span + PAD :][: 3 * count] for s in slots[0]]).astype(F32)
    table = (held[:, :count] + held[:, count : 2 * count] + held[:, 2 * count :]).reshape(
        len(slots[0]), layers, table_rows, f
    )
    own_up = table[0, :, len(smalls) :].reshape(layers, -1)
    natural = table[slot_blocks()]
    product_rows = [
        [
            rows_for_products(*(natural[:, layer, n].reshape(width) for n in pair))
            for pair in ((0, 1), (5, 6))
        ]
        for layer in range(layers)
    ]

    no_rows = jnp.zeros((PAD, f), BF16)
    saved = []
    turn = ()
    for layer in range(layers):
        last = layer + 1 == layers
        first_w = by_blocks(packs[layer][0], rows)
        joined_w, output_w = Columns(first_w, 3 * f), Columns(first_w, f, 3)
        products = []
        gains = [table[:, layer, n] for n in range(len(smalls))]
        own = table[0, layer]
        zero = jnp.zeros((heads_local, HEAD_DIM), F32)
        joined_bias = jnp.stack(
            (own[2].reshape(heads_local, HEAD_DIM), zero, own[3].reshape(heads_local, HEAD_DIM)), axis=1
        ).reshape(3 * f)
        joined, kept = [], []
        for k in chunks:
            slots[k], _ = lax.optimization_barrier((slots[k], turn))
            normed_one, centred_one, inverse_one, product_one, hidden = norm_matmul(
                slots[k], residual[k], gains[0], gains[1], joined_w, joined_bias, product_rows[layer][0], False
            )
            joined.append(hidden)
            if layer == 0:
                joined[k] = after(joined[k], *first_slots[k])
            context, log_total = attend(k, joined, lengths, slopes)
            pair = column_sum(context, output_w, no_rows)
            turn = pair
            middle = residual[k] + ring_sum(pair)[:span] + own[4]
            slots[k] = gather_slots(shard_of(middle))
            kept.append([normed_one, centred_one, inverse_one, context, log_total, middle])
        up_w = Columns(by_blocks(after(packs[layer][1], turn), rows), up_weight.shape[2])
        for k in chunks:
            middle = kept[k].pop()
            slots[k], _ = lax.optimization_barrier((slots[k], turn))
            normed_two, centred_two, inverse_two, product_two, upper, activated = norm_matmul(
                slots[k], middle, gains[5], gains[6], up_w, own_up[layer], product_rows[layer][1], True
            )
            if k == 0:
                down_w = Columns(by_blocks(after(packs[layer][2], upper), rows), down_weight.shape[1])
            turn = (activated,)
            if not last:
                pair = column_sum(activated, down_w, no_rows)
                turn = pair
                residual[k] = middle + ring_sum(pair)[:span] + own[7]
                slots[k] = gather_slots(shard_of(residual[k]))
            kept[k] += [normed_two, centred_two, inverse_two, upper, activated, middle]
        weights.append((joined_w, output_w, up_w, down_w))
        saved.append((joined, joined_bias, kept, product_one, product_two))

    weight_terms = [None] * layers
    small_terms = [None] * layers
    result, last_pairs, back_middle = ([None] * CHUNKS for _ in range(3))
    last_down_w = weights[-1][3]
    middle_grad = [None] * CHUNKS
    passed_one = [None] * CHUNKS

    def term(pieces):
        return added(
            [jnp.einsum("td,tn->dn", a, b, preferred_element_type=F32) for a, b in pieces]
        ).astype(BF16)

    for layer in reversed(range(layers)):
        joined, joined_bias, kept, product_one, product_two = saved[layer]
        joined_w, output_w, up_w, down_w = weights[layer]
        own = table[0, layer]
        up_gain, up_shift = product_two[0] + product_two[1], product_two[2] + product_two[3]
        joined_gain, joined_shift = product_one[0] + product_one[1], product_one[2] + product_one[3]
        given = None
        middle_slots, smalls_of, down_ends, up_ends, joined_ends, output_ends = ([None] * CHUNKS for _ in range(6))
        for k in reversed(chunks):
            normed_two, centred_two, inverse_two, upper, activated, middle = kept[k][5:]
            down_bias_term = jnp.sum(gradient[k], axis=0)
            slots = first_slots[k]
            slots, _ = lax.optimization_barrier((slots, turn))
            low_gradient, upper_grad, extra, up_bias_term = hidden_back(
                slots, down_w, upper, up_gain, own_up[layer] + up_shift
            )
            pair = column_sum(upper_grad, up_w, extra)
            turn = pair
            down_ends[k] = (low_gradient, after(activated, pair))
            if layer == 0:
                last_active = after(saved[-1][2][k][9], pair)
                last_pairs[k] = column_sum(last_active, last_down_w, no_rows)
            normed_two_grad = ring_sum(pair)
            if layer == 0:
                normed_two_grad = after(normed_two_grad, last_pairs[k])
            if k == 0:
                down_term = term(down_ends)
                normed_two_grad = after(normed_two_grad, down_term)
                if layer + 1 < layers:
                    normed_two_grad = after(normed_two_grad, joint_sum, up_pair[1])
                    joint_pair = swapped(joint_sum)
                    weight_terms[layer + 1] = [joint_pair, up_pair, down_pair]
                down_sum = scatter_weight(down_term)
            passed_two, gain_two_term, shift_two_term = norm_backward(
                normed_two_grad, centred_two, inverse_two, own[5], width
            )
            middle_grad[k] = gradient[k] + passed_two
            output_bias_term = jnp.sum(middle_grad[k], axis=0)
            smalls_of[k] = [output_bias_term, gain_two_term, shift_two_term, down_bias_term, up_bias_term]
            up_ends[k] = (normed_two, after(upper_grad, middle_grad[k]))
            middle_slots[k] = gather_slots(middle_grad[k].astype(BF16))
        for k in reversed(chunks):
            normed_one, centred_one, inverse_one, context, log_total = kept[k][:5]
            slots = middle_slots[k]
            slots, _ = lax.optimization_barrier((slots, turn))
            if k == 0:
                up_term = term(up_ends)
                slots, _ = lax.optimization_barrier((slots, (up_term, down_sum)))
                up_sum = scatter_weight(up_term)
                down_pair = swapped(down_sum)
            low_middle, context_grad = gather_matmul(slots, output_w)
            if layer == 0:
                back_middle[k] = swap_roles(after(middle_grad[k], low_middle))
                last_total = ring_sum(after(last_pairs[k], slots))
                result[k] = saved[-1][2][k][10] + last_total[:span] + table[0, layers - 1, 7]
            joined_grad, given = attend_back(
                k, joined, given, context_grad, log_total, lengths, slopes
            )
            wide_grad = joined_grad.astype(F32)
            first_sum = jnp.sum(wide_grad * joined_gain, axis=1)
            second_sum = jnp.sum(
                wide_grad * (joined[k].astype(F32) - (joined_bias + joined_shift)), axis=1
            )
            joined_ends[k] = (normed_one, joined_grad)
            output_ends[k] = (low_middle, context)
            if k == 0 and layer == 0:
                first_term = jnp.concatenate([term(joined_ends), term(output_ends)], axis=1)
                first_sum = after(first_sum, first_term, result[k], back_middle, weight_terms[-1][0][1])
                back_result = [swap_roles(r) for r in result]
            pair = column_sum(joined_grad, joined_w, sums_rows(first_sum, second_sum, f))
            turn = pair
            normed_one_grad = ring_sum(pair)
            if k == 0:
                up_pair = swapped(up_sum)
            if k == 0 and layer == 0:
                normed_one_grad = after(
                    normed_one_grad, down_pair[1], back_result
                )
            if k == 0 and layer > 0:
                joined_ends[0] = (normed_one, after(joined_grad, pair))
                output_ends[0] = (low_middle, after(context, pair))
                first_term = jnp.concatenate([term(joined_ends), term(output_ends)], axis=1)
                normed_one_grad = after(normed_one_grad, first_term, up_sum, down_pair[1])
            if k == 0:
                joint_sum = scatter_weight(first_term)
            joined_bias_term = jnp.sum(joined_grad.astype(F32), axis=0).reshape(heads_local, 3, HEAD_DIM)
            passed_one[k], gain_one_term, shift_one_term = norm_backward(
                normed_one_grad, centred_one, inverse_one, own[0], width
            )
            gradient[k] = middle_grad[k] + passed_one[k]
            if layer > 0:
                first_slots[k] = gather_slots(gradient[k].astype(BF16))
            smalls_of[k] = jnp.concatenate(
                [
                    t.reshape(-1, f)
                    for t in (
                        gain_one_term,
                        shift_one_term,
                        joined_bias_term[:, 0],
                        joined_bias_term[:, 2],
                        *smalls_of[k],
                    )
                ],
                axis=0,
            )
        small_terms[layer] = added(smalls_of)
    back_passed = [swap_roles(p.astype(BF16)) for p in passed_one]
    small = jnp.stack(small_terms)
    for axis in ("rh", "x"):
        size = lax.axis_size(axis)
        small = small + added(
            [lax.ppermute(small, axis, [(r, r ^ k) for r in range(size)]) for k in range(1, size)]
        )
    same = lax.axis_index("c") == lax.axis_index("x")
    small = jnp.where(same, small, partner(small))

    input_grad = jnp.concatenate(
        [m + after(p, small).astype(F32) for m, p in zip(back_middle, back_passed)],
        axis=0,
    )
    weight_terms[0] = [swapped(joint_sum), up_pair, down_pair]
    joined_out, output_out = unpack([t[0] for t in weight_terms], (False, True), (3 * f, f))
    (up_out,) = unpack([t[1] for t in weight_terms], (False,), (up_weight.shape[2],))
    (down_out,) = unpack([t[2] for t in weight_terms], (True,), (down_weight.shape[1],))

    return (
        jnp.concatenate(back_result, axis=0),
        input_grad,
        small[:, 0],
        small[:, 1],
        joined_out,
        small[:, 2],
        small[:, 3],
        output_out,
        small[:, 4],
        small[:, 5],
        small[:, 6],
        up_out,
        small[:, 8:].reshape(layers, -1),
        down_out,
        small[:, 7],
    )


def solution(mesh):
    rows, columns = mesh.devices.shape
    inner = Mesh(mesh.devices.reshape(rows // 2, 2, columns // 2, 2), ("rh", "c", "t", "x"))
    row, col = ("rh", "c"), ("t", "x")
    return jax.shard_map(
        on_device,
        mesh=inner,
        in_specs=(
            P(row, col),
            P(row, col),
            P(row),
            P(None, col),
            P(None, col),
            P(None, row, col),
            P(None, col),
            P(None, col),
            P(None, col, row),
            P(None, col),
            P(None, col),
            P(None, col),
            P(None, row, col),
            P(None, col),
            P(None, col, row),
            P(None, col),
        ),
        out_specs=(
            P(row, col),
            P(row, col),
            P(None, col),
            P(None, col),
            P(None, row, col),
            P(None, col),
            P(None, col),
            P(None, col, row),
            P(None, col),
            P(None, col),
            P(None, col),
            P(None, row, col),
            P(None, col),
            P(None, col, row),
            P(None, col),
        ),
        check_vma=False,
    )
```
